256 devices in a mesh: sub: 32 (over x, y, core), grp: 8 (over z).
Axes of the slice: x: 4, y: 4, z: 8, core: 2. Of those that a mesh axis runs over, the one named last changes fastest.
Arguments:
- residual: float32 [256, 1024, 256], P(('sub', 'grp')), may hold values from -6 to 6
- dscale: float32 [256, 1024], P(('sub', 'grp')), may hold values from 0.3 to 1
- local_inverse: bfloat16 [256, 1024, 1024], P(('sub', 'grp')), may hold values from -4 to 4
- coarse_basis: bfloat16 [256, 1024, 384], P(('sub', 'grp')), may hold values from -0.1875 to 0.1875
- block_counts: int32 [256], P(('sub', 'grp')), may hold values from 1 to 3, as said below
- block_index: int32 [256, 3], P(('sub', 'grp')), may hold values from 0 to 11, as said below
- level2_inverse: bfloat16 [32, 1536, 1536], P('sub', 'grp'), may hold values from -4 to 4
- level2_basis: bfloat16 [32, 1536, 1024], P('sub', 'grp'), may hold values from -0.15625 to 0.15625
- group_index: int32 [32, 8], P('sub'), may hold values from 0 to 31, as said below
- level3_inverse: bfloat16 [4096, 4096], P(('sub', 'grp')), may hold values from -4 to 4
Outputs:
- result: float32 [256, 1024, 256], P(('sub', 'grp'))
The draws below stay inside these ranges and needn't reach their ends.
Inputs may be any that keep to these rules, and one draw needn't show every extreme that they name: `block_counts`: each level-2 subdomain has at least one member with all 3 blocks live. `block_index`: the blocks of one subdomain name different level-2 blocks; before block_counts are applied, the subdomains of one level-2 subdomain name each of its blocks exactly 8 * 3 / 12 times. `group_index`: the blocks of one level-2 subdomain name different level-3 blocks; all level-2 subdomains together name each level-3 block exactly 32 * 8 / 32 times.
All inputs are finite; a program needn't handle non-finite values.
Results may differ from the reference program's by a relative error of at most 0.0035.
Values may be sent and summed in bfloat16 or wider, within the bound.
A program may use at most 64 MiB of HBM per device.

```python
import math
import jax
import jax.numpy as jnp
from jax import lax

NL = 1024
NRHS = 256
CB = 128
NCB = 3
NB2 = 12
MB2 = 8
NB3 = 32
SUBS = 256
GROUPS = 32
NC = 384
N2 = 1536
M2 = 1024
N3 = 4096
N_SUB = 32
N_GRP = 8


def dominant(key, count, order, low, high, spread, row_spread):
    keys = jax.random.split(key, 4)
    diagonal = jax.random.uniform(keys[0], (count, order), jnp.float32, low, high)
    normal_part = jnp.clip(jax.random.normal(keys[1], (count, order, order), jnp.float32), -4.0, 4.0)
    offdiag = normal_part * (spread / math.sqrt(order))
    row_scale = jnp.exp(jax.random.uniform(keys[3], (count, order, 1), jnp.float32, -row_spread, row_spread))
    identity = jnp.eye(order, dtype=jnp.float32)
    return (identity[None] * diagonal[:, None, :] + offdiag) * row_scale


def permuted(key, count, length):
    keys = jax.random.split(key, count)

    def one_perm(single):
        return jax.random.permutation(single, length)
    return jax.vmap(one_perm)(keys)


def draw_local_inverse(key, part):
    key = jax.random.fold_in(key, 11)
    matrix = dominant(key, SUBS, NL, 0.6, 1.4, 0.6, 0.0)
    return matrix.astype(jnp.bfloat16)


def draw_level2_inverse(key, part):
    key = jax.random.fold_in(key, 12)
    matrix = dominant(key, GROUPS, N2, 0.4, 1.0, 0.5, 0.0)
    return matrix.astype(jnp.bfloat16)


def draw_level3_inverse(key, part):
    key = jax.random.fold_in(key, 13)
    matrix = dominant(key, 1, N3, 0.1, 0.3, 0.1, 0.0)
    return matrix[0].astype(jnp.bfloat16)


def draw_block_counts(key, part):
    key = jax.random.fold_in(key, 21)
    count_key, pick_key = jax.random.split(key)
    members = SUBS // GROUPS
    counts = jax.random.randint(count_key, (GROUPS, members), 1, NCB + 1)
    chosen = jax.random.randint(pick_key, (GROUPS, 1), 0, members)
    filled = jnp.arange(members, dtype=jnp.int32)[None, :] == chosen
    return jnp.where(filled, NCB, counts).reshape(SUBS).astype(jnp.int32)


def draw_block_index(key, part):
    key = jax.random.fold_in(key, 22)
    members = SUBS // GROUPS
    repeats = members * NCB // NB2
    return permuted(key, GROUPS * repeats, NB2).reshape(SUBS, NCB).astype(jnp.int32)


def draw_group_index(key, part):
    key = jax.random.fold_in(key, 23)
    repeats = GROUPS * MB2 // NB3
    return permuted(key, repeats, NB3).reshape(GROUPS, MB2).astype(jnp.int32)


def shard_levels(rng, dims, cuts, least, top_value):
    level = 1.0
    for dim, blocks in cuts:
        draws = jax.random.uniform(jax.random.fold_in(jax.random.fold_in(rng, 6), dim), (blocks,), jnp.float32, least / len(cuts), top_value / len(cuts))
        level = level * jnp.repeat(jnp.exp(draws), dims[dim] // blocks).reshape((-1,) + (1,) * (len(dims) - 1 - dim))
    return level


def gaussian(own_key, extent, deviation, limit, shards=(), held_as=jnp.bfloat16):
    loudness = shard_levels(own_key, extent, shards, -0.22, 0.18) if shards else 1.0
    values = jax.random.normal(own_key, extent, jnp.float32) * deviation * loudness
    return jnp.minimum(jnp.maximum(values, -limit), limit).astype(held_as)


def setup_inputs(seed: int = 0) -> dict:
    splits = jax.random.split(jax.random.key(seed), 11)
    residual = gaussian(splits[0], (SUBS, NL, NRHS), 1.0, 6.0, ((0, 256),), jnp.float32)
    dscale = jnp.clip(0.3 + 0.7 * jax.random.uniform(splits[1], (SUBS, NL), jnp.float32) ** shard_levels(splits[1], (SUBS, NL), ((0, 256),), -0.2, 0.2), 0.3, 1.0)
    local_inverse = draw_local_inverse(jax.random.fold_in(splits[10], 71), 0)
    coarse_basis = gaussian(splits[3], (SUBS, NL, NC), NL ** -0.5, 0.1875, ((0, 256),))
    block_counts = draw_block_counts(jax.random.fold_in(splits[10], 71), 0)
    block_index = draw_block_index(jax.random.fold_in(splits[10], 71), 0)
    level2_inverse = draw_level2_inverse(jax.random.fold_in(splits[10], 71), 0)
    level2_basis = gaussian(splits[7], (GROUPS, N2, M2), N2 ** -0.5, 0.15625, ((0, 32), (1, 8)))
    group_index = draw_group_index(jax.random.fold_in(splits[10], 71), 0)
    level3_inverse = draw_level3_inverse(jax.random.fold_in(splits[10], 71), 0)
    return dict(residual=residual, dscale=dscale, local_inverse=local_inverse, coarse_basis=coarse_basis, block_counts=block_counts, block_index=block_index, level2_inverse=level2_inverse, level2_basis=level2_basis, group_index=group_index, level3_inverse=level3_inverse)


HIGHEST_PRECISION = lax.Precision.HIGHEST


def first_level(inputs):
    inverse, basis_rows, vector = inputs
    solved = jnp.dot(inverse, vector, preferred_element_type=jnp.float32)
    coarse = lax.dot_general(basis_rows, vector, (((0,), (0,)), ((), ())), preferred_element_type=jnp.float32)
    return solved, coarse


def lift_up(inputs):
    basis_rows, vector = inputs
    return jnp.dot(basis_rows, vector, preferred_element_type=jnp.float32)


def pick_blocks(inputs):
    solution, indices = inputs
    return solution.reshape(NB2, CB, NRHS)[indices]


def reference(residual, dscale, local_inverse, coarse_basis, block_counts, block_index, level2_inverse, level2_basis, group_index, level3_inverse):
    weighted = (dscale[:, :, None] * residual).astype(jnp.bfloat16)
    local_part, coarse = lax.map(first_level, (local_inverse, coarse_basis, weighted))
    active = jnp.arange(NCB, dtype=jnp.int32)[None, :] < block_counts[:, None]
    blocks = coarse.reshape(SUBS, NCB, CB, NRHS) * active[:, :, None, None].astype(jnp.float32)
    slot_table = (block_index[:, :, None] == jnp.arange(NB2, dtype=jnp.int32)[None, None, :]) & active[:, :, None]
    slot_table = slot_table.astype(jnp.float32).reshape(GROUPS, N_GRP, NCB, NB2)
    level2_rhs = jnp.einsum("gmkj,gmkcr->gjcr", slot_table, blocks.reshape(GROUPS, N_GRP, NCB, CB, NRHS), precision=HIGHEST_PRECISION)
    level2_b = level2_rhs.reshape(GROUPS, N2, NRHS).astype(jnp.bfloat16)
    level2_local, level2_coarse = lax.map(first_level, (level2_inverse, level2_basis, level2_b))
    group_table = (group_index[:, :, None] == jnp.arange(NB3, dtype=jnp.int32)[None, None, :]).astype(jnp.float32)
    level3_rhs = jnp.einsum("gjb,gjcr->bcr", group_table, level2_coarse.reshape(GROUPS, MB2, CB, NRHS), precision=HIGHEST_PRECISION)
    level3_b = level3_rhs.reshape(N3, NRHS).astype(jnp.bfloat16)
    level3_solution = jnp.dot(level3_inverse, level3_b, preferred_element_type=jnp.float32).astype(jnp.bfloat16)
    level3_taken = level3_solution.reshape(NB3, CB, NRHS)[group_index].reshape(GROUPS, M2, NRHS)
    level2_solution = (level2_local + lax.map(lift_up, (level2_basis, level3_taken))).astype(jnp.bfloat16)
    chosen = lax.map(pick_blocks, (level2_solution, block_index.reshape(GROUPS, N_GRP * NCB)))
    chosen = chosen.reshape(SUBS, NCB, CB, NRHS) * active[:, :, None, None].astype(jnp.bfloat16)
    coarse_part = lax.map(lift_up, (coarse_basis, chosen.reshape(SUBS, NC, NRHS)))
    total = dscale[:, :, None] * (local_part + coarse_part)
    assembled = total.reshape(N_SUB, N_GRP, NL, NRHS)
    face_width = NL // 8
    lower_grp = assembled[:, :, 0:face_width]
    upper_grp = assembled[:, :, face_width:2 * face_width]
    lower_sub = assembled[:, :, 2 * face_width:3 * face_width]
    upper_sub = assembled[:, :, 3 * face_width:4 * face_width]
    empty_grp = jnp.zeros_like(lower_grp[:, :1])
    empty_sub = jnp.zeros_like(lower_sub[:1])
    below_grp = jnp.concatenate([empty_grp, upper_grp[:, :-1]], axis=1)
    above_grp = jnp.concatenate([lower_grp[:, 1:], empty_grp], axis=1)
    below_sub = jnp.concatenate([empty_sub, upper_sub[:-1]], axis=0)
    above_sub = jnp.concatenate([lower_sub[1:], empty_sub], axis=0)
    result = jnp.concatenate([lower_grp + below_grp, upper_grp + above_grp, lower_sub + below_sub, upper_sub + above_sub, assembled[:, :, 4 * face_width:]], axis=2)
    return result.reshape(SUBS, NL, NRHS)
```

```python
import functools

import jax
import jax.numpy as jnp
from jax import lax
from jax.experimental import pallas as pl
from jax.experimental.pallas import tpu as pltpu
from jax.sharding import PartitionSpec as P

NS = 32
NG = 8
NL = 1024
NR = 256
CB = 128
NCB = 3
NB2 = 12
MB2 = 8
NB3 = 32
SL = CB // NG
OWN2 = NB2 * CB // NG
HB = CB // 2
NH = OWN2 // HB
NCH = 1
W = NR // NCH
NSUB = 3

MESH = pl.DeviceIdType.MESH
BF = jnp.bfloat16
F32 = jnp.float32


def dot(a, b):
    return jnp.dot(a, b, preferred_element_type=F32)


def dot_t(a, b):
    return lax.dot_general(a, b, (((0,), (0,)), ((), ())), preferred_element_type=F32)


def kernel(
    cnt_s, bidx_s, gidx_s, dsc_v, res_h, linv_h, cbas_h, l2inv_h, l2bas_h, l3inv_h,
    out_ref,
    res, linv, cbas, l2inv, l2bas, l3inv, load_sem,
    dcol, wgt, local, perm, tstage, tsend, tile, t_ss, t_rs,
    meta_v, meta_s, m_ss, m_rs, ms_sem, tab, gtab,
    blocks, b_ss, b_rs,
    rhs2, l2loc, part, d_recv, d_ss, d_rs,
    ssum, dense, e_recv, e_ss, e_rs,
    xall, f_ss, f_rs,
    hsend, h_recv, h_ss, h_rs,
    yall, i_ss, i_rs,
    picked, lifted, j_ss, j_rs,
    sol2, l_ss, l_rs,
    chosen, fsend, f_recv, n_ss, n_rs,
):
    s, g = lax.axis_index("sub"), lax.axis_index("grp")

    loads = [
        pltpu.make_async_copy(src, dst, load_sem.at[n])
        for n, (src, dst) in enumerate(
            [(res_h, res), (cbas_h, cbas), (linv_h, linv), (l2bas_h, l2bas), (l2inv_h, l2inv),
             (l3inv_h, l3inv)]
        )
    ]
    for load in loads:
        load.start()

    bar = pltpu.get_barrier_semaphore()

    def hail_z(i, c):
        pl.semaphore_signal(bar, inc=1, device_id=(s, lax.rem(g + i, NG)), device_id_type=MESH)
        return c

    def hail_p(i, c):
        pl.semaphore_signal(bar, inc=1, device_id=(lax.rem(s + i, NS), g), device_id_type=MESH)
        return c

    lax.fori_loop(1, NG, hail_z, 0)
    lax.fori_loop(1, NS, hail_p, 0)

    def remote(src, dst, ss, rs, dev):
        return pltpu.make_async_remote_copy(
            src_ref=src, dst_ref=dst, send_sem=ss, recv_sem=rs, device_id=dev, device_id_type=MESH
        )

    def z_copy(i, make, ss, rs):
        t = lax.rem(g + i, NG)
        src, dst = make(t)
        return remote(src, dst, ss.at[i], rs.at[i], (s, t))

    def p_copy(i, make, ss, rs):
        t = lax.rem(s + i, NS)
        src, dst = make(t)
        return remote(src, dst, ss.at[i], rs.at[i], (t, g))

    def start_all(copy, n, make, ss, rs):
        def f(i, c):
            copy(i, make, ss, rs).start()
            return c

        lax.fori_loop(1, n, f, 0)

    def recv_all(copy, n, make, ss, rs):
        def f(i, c):
            copy(i, make, ss, rs).wait_recv()
            return c

        lax.fori_loop(1, n, f, 0)

    def sent_all(copy, n, make, ss, rs):
        def f(i, c):
            copy(i, make, ss, rs).wait_send()
            return c

        lax.fori_loop(1, n, f, 0)

    def ring_copy(way, step, q, slot, ss, rs):
        if way == 0:
            o, t = lax.rem(g - step + NG, NG), lax.rem(g + 1, NG)
        else:
            o, t = lax.rem(g + step, NG), lax.rem(g + NG - 1, NG)
        ref = slot(o, q)
        return remote(ref, ref, ss.at[way, step, q], rs.at[way, step, q], (s, t))

    half = NG // 2

    def ring_steps():
        for step in range(half):
            for q in range(NSUB):
                for way in range(2):
                    if step == half - 1 and (q % 2 != way):
                        continue
                    yield step, q, way

    def ring(slot, ss, rs):
        for step, q, way in ring_steps():
            if step > 0:
                ring_copy(way, step - 1, q, slot, ss, rs).wait_recv()
            ring_copy(way, step, q, slot, ss, rs).start()

    def ring_end(slot, ss, rs):
        for q in range(NSUB):
            for way in range(2):
                last = half - 1 if q % 2 == way else half - 2
                ring_copy(way, last, q, slot, ss, rs).wait_recv()

    def ring_sent(slot, ss, rs):
        for step, q, way in ring_steps():
            ring_copy(way, step, q, slot, ss, rs).wait_send()

    def spread(i, c):
        at = pl.ds(pl.multiple_of(i * 128, 128), 128)
        row = jnp.broadcast_to(dsc_v[0:1, at], (128, 128))
        dcol[at, :] = row.T
        return c

    lax.fori_loop(0, NL // 128, spread, 0)
    loads[0].wait()

    def weigh(i, c):
        at = pl.ds(pl.multiple_of(i * 128, 128), 128)
        d = dcol[at, :]
        for n in range(NR // 128):
            cols = slice(n * 128, n * 128 + 128)
            wgt[at, cols] = (res[at, cols] * d).astype(BF)
        return c

    lax.fori_loop(0, NL // 128, weigh, 0)

    lane = lax.broadcasted_iota(jnp.int32, (1, 128), 1)
    meta_v[pl.ds(g, 1), :] = jnp.where(
        lane == 0, bidx_s[0, 0], jnp.where(lane == 1, bidx_s[0, 1], bidx_s[0, 2])
    )
    pl.semaphore_wait(bar, NG - 1 + NS - 1)

    def m_make(t):
        return meta_v.at[pl.ds(g, 1)], meta_v.at[pl.ds(g, 1)]

    start_all(z_copy, NG, m_make, m_ss, m_rs)

    loads[1].wait()
    for c in range(NCH):
        for k in range(NCB):
            v = dot_t(cbas[:, k * CB : (k + 1) * CB], wgt[:, c * W : (c + 1) * W])
            live = (cnt_s[0] > k).astype(F32)
            blocks[c, pl.ds((g * NCB + k) * 2, 2)] = (v * live).astype(BF).reshape(2, HB, W)

    def b_slot(c):
        return lambda o, q: blocks.at[c, pl.ds((o * NCB + q) * 2, 2)]

    for c in range(NCH):
        ring(b_slot(c), b_ss.at[c], b_rs.at[c])

    loads[2].wait()

    def local_tile(i, c):
        at = pl.ds(pl.multiple_of(i * 256, 256), 256)
        local[at, :] = dot(linv[at, :], wgt[...])
        return c

    lax.fori_loop(0, NL // 256, local_tile, 0)

    recv_all(z_copy, NG, m_make, m_ss, m_rs)
    to_s = pltpu.make_async_copy(meta_v, meta_s, ms_sem)
    to_s.start()
    to_s.wait()

    def name_pairs(j, c):
        lo = jnp.int32(NG * NCB - 1)
        hi = jnp.int32(0)
        for p in range(NG * NCB - 1, -1, -1):
            lo = jnp.where(meta_s[p // NCB, p % NCB] == j, p, lo)
        for p in range(NG * NCB):
            hi = jnp.where(meta_s[p // NCB, p % NCB] == j, p, hi)
        tab[0, j] = lo
        tab[1, j] = hi
        return c

    lax.fori_loop(0, NB2, name_pairs, 0)

    def name_slots(b, c):
        at = jnp.int32(0)
        has = jnp.int32(0)
        for j in range(MB2):
            hit = gidx_s[0, j] == b
            at = jnp.where(hit, j, at)
            has = jnp.where(hit, 1, has)
        gtab[0, b] = at
        gtab[1, b] = has
        return c

    lax.fori_loop(0, NB3, name_slots, 0)

    loads[5].wait()
    for q in range(4):
        tstage[q * SL : (q + 1) * SL, :] = l3inv[:, q * 1024 : (q + 1) * 1024]

    def fill_perm(b, c):
        k = lax.broadcasted_iota(jnp.int32, (128, 1024), 0)
        n = lax.broadcasted_iota(jnp.int32, (128, 1024), 1)
        want = (k // SL) * 128 + b * SL + k % SL
        perm[pl.ds(pl.multiple_of(b * 128, 128), 128), :] = jnp.where(n == want, 1.0, 0.0).astype(BF)
        return c

    lax.fori_loop(0, 8, fill_perm, 0)
    moved = dot(tstage[...], perm[...]).astype(BF)
    for m in range(NG):
        for q in range(4):
            tsend[m, :, q * 128 : (q + 1) * 128] = moved[q * SL : (q + 1) * SL, m * 128 : (m + 1) * 128]

    def t_make(t):
        return tsend.at[t], tile.at[g]

    tile[g] = tsend[g]
    start_all(z_copy, NG, t_make, t_ss, t_rs)

    loads[3].wait()
    loads[4].wait()

    def own_rhs(c):
        ring_end(b_slot(c), b_ss.at[c], b_rs.at[c])
        pieces = []
        for i in range(3):
            h = g * 3 + i
            j, low = h // 2, lax.rem(h, 2)
            v = blocks[c, tab[0, j] * 2 + low].astype(F32) + blocks[c, tab[1, j] * 2 + low].astype(F32)
            pieces.append(v.astype(BF))
        return jnp.concatenate(pieces, axis=0)

    def d_make(c):
        return lambda t: (part.at[c, :, t], d_recv.at[c, g])

    for c in range(NCH):
        mine = own_rhs(c)
        for n in range(MB2 // 2):
            v = dot_t(l2bas[:, n * 256 : (n + 1) * 256], mine).astype(BF)
            part[c, 2 * n : 2 * n + 2] = v.reshape(2, NG, SL, W)
        start_all(z_copy, NG, d_make(c), d_ss.at[c], d_rs.at[c])
        for j in range(MB2):
            d_recv[c, g, j] = part[c, j, g]

    def sum_pairs(c):
        def f(j, x):
            for low in range(2):
                v = blocks[c, tab[0, j] * 2 + low].astype(F32) + blocks[c, tab[1, j] * 2 + low].astype(F32)
                at = pl.ds(pl.multiple_of(j * CB + low * HB, HB), HB)
                rhs2[at, c * W : (c + 1) * W] = v.astype(BF)
            return x

        lax.fori_loop(0, NB2, f, 0)

    for c in range(NCH):
        sum_pairs(c)
    l2loc[...] = dot(l2inv[...], rhs2[...])

    def e_make(c):
        return lambda t: (dense.at[c, t], e_recv.at[c, s])

    def f_make(c):
        return lambda t: (xall.at[c, s], xall.at[c, s])

    def h_make(c):
        return lambda t: (hsend.at[c, t], h_recv.at[c, g])

    def i_make(c):
        return lambda t: (yall.at[c, s], yall.at[c, s])

    def j_make(c):
        return lambda t: (picked.at[c], lifted.at[c, :, g])

    def l_slot(c):
        return lambda o, q: sol2.at[c, o * NH + q]

    def phase_e(c):
        recv_all(z_copy, NG, d_make(c), d_ss.at[c], d_rs.at[c])
        for j in range(MB2):
            v = d_recv[c, 0, j].astype(F32)
            for m in range(1, NG):
                v = v + d_recv[c, m, j].astype(F32)
            ssum[c, j] = v

        def f(b, x):
            dense[c, b] = (ssum[c, gtab[0, b]] * gtab[1, b].astype(F32)).astype(BF)
            return x

        lax.fori_loop(0, NB3, f, 0)
        start_all(p_copy, NS, e_make(c), e_ss.at[c], e_rs.at[c])
        e_recv[c, s] = dense[c, s]

    def phase_f(c):
        recv_all(p_copy, NS, e_make(c), e_ss.at[c], e_rs.at[c])

        def f(b, v):
            return v + e_recv[c, b].astype(F32)

        xall[c, s] = lax.fori_loop(0, NS, f, jnp.zeros((SL, W), F32)).astype(BF)
        start_all(p_copy, NS, f_make(c), f_ss.at[c], f_rs.at[c])

    def phase_h(c):
        if c == 0:
            recv_all(z_copy, NG, t_make, t_ss, t_rs)
        recv_all(p_copy, NS, f_make(c), f_ss.at[c], f_rs.at[c])
        v = dot(tile[...].reshape(CB, NB3 * SL), xall[c].reshape(NB3 * SL, W))
        hsend[c] = v.astype(BF).reshape(NG, SL, W)
        start_all(z_copy, NG, h_make(c), h_ss.at[c], h_rs.at[c])
        h_recv[c, g] = hsend[c, g]

    def phase_i(c):
        recv_all(z_copy, NG, h_make(c), h_ss.at[c], h_rs.at[c])
        v = h_recv[c, 0].astype(F32)
        for m in range(1, NG):
            v = v + h_recv[c, m].astype(F32)
        yall[c, s] = v.astype(BF)
        start_all(p_copy, NS, i_make(c), i_ss.at[c], i_rs.at[c])

    def phase_j(c):
        recv_all(p_copy, NS, i_make(c), i_ss.at[c], i_rs.at[c])
        for j in range(MB2):
            v = yall[c, gidx_s[0, j]]
            picked[c, j] = v
            lifted[c, j, g] = v
        start_all(z_copy, NG, j_make(c), j_ss.at[c], j_rs.at[c])

    def phase_l(c):
        recv_all(z_copy, NG, j_make(c), j_ss.at[c], j_rs.at[c])
        cols = slice(c * W, (c + 1) * W)
        v = l2loc[:, cols] + dot(l2bas[...], lifted[c].reshape(MB2 * CB, W))
        sol2[c, pl.ds(g * NH, NH)] = v.astype(BF).reshape(NH, HB, W)
        ring(l_slot(c), l_ss.at[c], l_rs.at[c])

    def n_copy(c, f):
        dev = (
            (s, lax.rem(g + NG - 1, NG)),
            (s, lax.rem(g + 1, NG)),
            (lax.rem(s + NS - 1, NS), g),
            (lax.rem(s + 1, NS), g),
        )[f]
        return remote(fsend.at[c, f], f_recv.at[c, f ^ 1], n_ss.at[c, f], n_rs.at[c, f ^ 1], dev)

    def total_rows(c, lo, n):
        v = dot(cbas[lo : lo + n, :], chosen[c])
        cols = slice(c * W, (c + 1) * W)
        v = v + local[lo : lo + n, cols]
        d = dcol[lo : lo + n, :]
        if W > 128:
            d = jnp.concatenate([d] * (W // 128), axis=1)
        return v * d

    def phase_n(c):
        ring_end(l_slot(c), l_ss.at[c], l_rs.at[c])
        for k in range(NCB):
            for low in range(2):
                v = sol2[c, bidx_s[0, k] * 2 + low].astype(F32) * (cnt_s[0] > k).astype(F32)
                at = k * CB + low * HB
                chosen[c, at : at + HB, :] = v.astype(BF)
        cols = slice(c * W, (c + 1) * W)
        for f in range(4):
            v = total_rows(c, f * CB, CB)
            out_ref[f * CB : (f + 1) * CB, cols] = v
            fsend[c, f] = v.astype(BF)
            n_copy(c, f).start()
        for f in range(2, 4):
            out_ref[f * 256 : (f + 1) * 256, cols] = total_rows(c, f * 256, 256)

    def phase_o(c):
        cols = slice(c * W, (c + 1) * W)
        inside = (g > 0, g < NG - 1, s > 0, s < NS - 1)
        for f in range(4):
            n_copy(c, f ^ 1).wait_recv()
            at = slice(f * CB, (f + 1) * CB)
            v = f_recv[c, f].astype(F32) * inside[f].astype(F32)
            out_ref[at, cols] = out_ref[at, cols] + v

    for phase in (phase_e, phase_f, phase_h, phase_i, phase_j, phase_l, phase_n, phase_o):
        for c in range(NCH):
            phase(c)

    sent_all(z_copy, NG, m_make, m_ss, m_rs)
    sent_all(z_copy, NG, t_make, t_ss, t_rs)
    for c in range(NCH):
        ring_sent(b_slot(c), b_ss.at[c], b_rs.at[c])
        sent_all(z_copy, NG, d_make(c), d_ss.at[c], d_rs.at[c])
        sent_all(p_copy, NS, e_make(c), e_ss.at[c], e_rs.at[c])
        sent_all(p_copy, NS, f_make(c), f_ss.at[c], f_rs.at[c])
        sent_all(z_copy, NG, h_make(c), h_ss.at[c], h_rs.at[c])
        sent_all(p_copy, NS, i_make(c), i_ss.at[c], i_rs.at[c])
        sent_all(z_copy, NG, j_make(c), j_ss.at[c], j_rs.at[c])
        ring_sent(l_slot(c), l_ss.at[c], l_rs.at[c])
        for f in range(4):
            n_copy(c, f).wait_send()


def local(
    residual,
    dscale,
    local_inverse,
    coarse_basis,
    block_counts,
    block_index,
    level2_inverse,
    level2_basis,
    group_index,
    level3_inverse,
):
    vm = pltpu.VMEM
    dma = pltpu.SemaphoreType.DMA
    smem = pl.BlockSpec(memory_space=pltpu.SMEM)
    vmem = pl.BlockSpec(memory_space=pltpu.VMEM)
    hbm = pl.BlockSpec(memory_space=pl.ANY)
    ring_sem = dma((NCH, 2, NG // 2, NSUB))
    z_sem = dma((NCH, NG))
    p_sem = dma((NCH, NS))
    scratch = [
        vm((NL, NR), F32), vm((NL, NL), BF), vm((NL, NCB * CB), BF), vm((OWN2, NB2 * CB), BF),
        vm((OWN2, MB2 * CB), BF), vm((SL, NB3 * CB), BF), dma((6,)),
        vm((NL, 128), F32), vm((NL, NR), BF), vm((NL, NR), F32), vm((1024, 1024), BF),
        vm((4 * SL, 1024), BF), vm((NG, SL, NB3 * SL), BF), vm((NG, SL, NB3 * SL), BF),
        dma((NG,)), dma((NG,)),
        vm((NG, 128), jnp.int32), pltpu.SMEM((NG, 128), jnp.int32), dma((NG,)), dma((NG,)),
        dma(()), pltpu.SMEM((2, NB2), jnp.int32), pltpu.SMEM((2, NB3), jnp.int32),
        vm((NCH, NG * NCB * 2, HB, W), BF), ring_sem, ring_sem,
        vm((NB2 * CB, NR), BF), vm((OWN2, NR), F32), vm((NCH, MB2, NG, SL, W), BF),
        vm((NCH, NG, MB2, SL, W), BF), z_sem, z_sem,
        vm((NCH, MB2, SL, W), F32), vm((NCH, NB3, SL, W), BF), vm((NCH, NS, SL, W), BF), p_sem, p_sem,
        vm((NCH, NB3, SL, W), BF), p_sem, p_sem,
        vm((NCH, NG, SL, W), BF), vm((NCH, NG, SL, W), BF), z_sem, z_sem,
        vm((NCH, NB3, SL, W), BF), p_sem, p_sem,
        vm((NCH, MB2, SL, W), BF), vm((NCH, MB2, NG, SL, W), BF), z_sem, z_sem,
        vm((NCH, NG * NH, HB, W), BF), ring_sem, ring_sem,
        vm((NCH, NCB * CB, W), BF), vm((NCH, 4, CB, W), BF), vm((NCH, 4, CB, W), BF),
        dma((NCH, 4)), dma((NCH, 4)),
    ]
    out = pl.pallas_call(
        kernel,
        out_shape=jax.ShapeDtypeStruct((NL, NR), F32),
        in_specs=[smem, smem, smem, vmem] + [hbm] * 6,
        out_specs=vmem,
        scratch_shapes=scratch,
        name="bddc",
        compiler_params=pltpu.CompilerParams(
            collective_id=0, has_side_effects=True, vmem_limit_bytes=48 << 20
        ),
    )(
        block_counts, block_index, group_index, dscale, residual[0], local_inverse[0],
        coarse_basis[0], level2_inverse[0], level2_basis[0], level3_inverse,
    )
    return out[None]


def solution(mesh):
    return jax.shard_map(
        local,
        mesh=mesh,
        in_specs=(
            P(("sub", "grp"), None, None),
            P(("sub", "grp"), None),
            P(("sub", "grp"), None, None),
            P(("sub", "grp"), None, None),
            P(("sub", "grp")),
            P(("sub", "grp"), None),
            P("sub", "grp", None),
            P("sub", "grp", None),
            P("sub", None),
            P(("sub", "grp"), None),
        ),
        out_specs=P(("sub", "grp"), None, None),
        check_vma=False,
    )
```

```python
import functools

import jax
import jax.numpy as jnp
from jax import lax
from jax.experimental import pallas as pl
from jax.experimental.pallas import tpu as pltpu
from jax.sharding import PartitionSpec as P

NS = 32
NG = 8
NL = 1024
NR = 256
CB = 128
NCB = 3
NB2 = 12
MB2 = 8
NB3 = 32
SL = CB // NG
OWN2 = NB2 * CB // NG
HB = CB // 2
NH = OWN2 // HB
NCH = 1
W = NR // NCH
PJ = 2

ORDER = (
    "b0", "w0", "w0", "w0", "w0", "w0", "b0", "w0", "w0", "w0", "d0", "q0", "e0", "t0", "f0", "a0",
    "h0", "a0", "i0", "j0", "g0", "s0", "k0", "l0", "l0", "n0", "r0", "o0",
)

MESH = pl.DeviceIdType.MESH
BF = jnp.bfloat16
F32 = jnp.float32


def dot(a, b):
    return jnp.dot(a, b, preferred_element_type=F32)


def dot_t(a, b):
    return lax.dot_general(a, b, (((0,), (0,)), ((), ())), preferred_element_type=F32)


def kernel(
    cnt_h, bidx_h, gidx_h, dsc_h, res_h, linv_h, cbas_h, l2inv_h, l2bas_h, l3inv_h,
    out_ref,
    cnt_s, bidx_s, gidx_s, dsc_v, res, linv, cbas, l2inv, l2bas, l3inv, load_sem,
    dcol, wgt, local, perm, tstage, tsend, tile, t_ss, t_rs,
    ctab, gtab,
    crs, own, b_stage, b_recv, b_ss, b_rs,
    rhs2, a_ss, a_rs, l2loc, part, d_stage, d_recv, d_ss, d_rs,
    ssum, dense, e_recv, e_ss, e_rs,
    xall, f_ss, f_rs,
    hsend, h_recv, h_ss, h_rs,
    yall, i_ss, i_rs,
    lifted, j_ss, j_rs,
    sol2, l_ss, l_rs,
    chosen, fsend, f_recv, n_ss, n_rs,
):
    s, g = lax.axis_index("sub"), lax.axis_index("grp")

    loads = [
        pltpu.make_async_copy(src, dst, load_sem.at[n])
        for n, (src, dst) in enumerate(
            [(res_h, res), (cbas_h, cbas), (linv_h, linv), (l2bas_h, l2bas), (l2inv_h, l2inv),
             (l3inv_h, l3inv), (dsc_h, dsc_v), (cnt_h, cnt_s), (bidx_h, bidx_s), (gidx_h, gidx_s)]
        )
    ]
    for n in (6, 7, 8, 9, 0, 1, 2, 3, 4, 5):
        loads[n].start()

    bar = pltpu.get_barrier_semaphore()

    def hail_z(i, c):
        pl.semaphore_signal(bar, inc=1, device_id=(s, lax.rem(g + i, NG)), device_id_type=MESH)
        return c

    def hail_p(i, c):
        pl.semaphore_signal(bar, inc=1, device_id=(lax.rem(s + i, NS), g), device_id_type=MESH)
        return c

    lax.fori_loop(1, NG, hail_z, 0)
    lax.fori_loop(1, NS, hail_p, 0)

    def remote(src, dst, ss, rs, dev):
        return pltpu.make_async_remote_copy(
            src_ref=src, dst_ref=dst, send_sem=ss, recv_sem=rs, device_id=dev, device_id_type=MESH
        )

    def z_copy(i, make, ss, rs):
        t = lax.rem(g + i, NG)
        src, dst = make(t)
        return remote(src, dst, ss.at[i], rs.at[i], (s, t))

    def p_copy(i, make, ss, rs):
        t = lax.rem(s + i, NS)
        src, dst = make(t)
        return remote(src, dst, ss.at[i], rs.at[i], (t, g))

    def start_all(copy, n, make, ss, rs):
        def f(i, c):
            copy(i, make, ss, rs).start()
            return c

        lax.fori_loop(1, n, f, 0)

    def recv_all(copy, n, make, ss, rs):
        def f(i, c):
            copy(i, make, ss, rs).wait_recv()
            return c

        lax.fori_loop(1, n, f, 0)

    def sent_all(copy, n, make, ss, rs):
        def f(i, c):
            copy(i, make, ss, rs).wait_send()
            return c

        lax.fori_loop(1, n, f, 0)

    sign = (1, -1)

    def away(n):
        return lax.rem(g + n + NG, NG)

    def kinds(kind, count):
        for p in range(count):
            for way in range(2):
                if kind != 3 or p % 2 == way:
                    yield p, way

    def ag_copy(kind, way, p, slot, ss, rs):
        o = g if kind < 2 else away(-2 * sign[way])
        ref = slot(o, p)
        to = away(sign[way] * (1, 2, 1, 2)[kind])
        return remote(ref, ref, ss.at[kind, way, p], rs.at[kind, way, p], (s, to))

    def gather(count, slot, ss, rs):
        for kind in (1, 0):
            for p, way in kinds(kind, count):
                ag_copy(kind, way, p, slot, ss, rs).start()
        yield
        for p, way in kinds(1, count):
            ag_copy(1, way, p, slot, ss, rs).wait_recv()
            ag_copy(2, way, p, slot, ss, rs).start()
            if p % 2 == way:
                ag_copy(3, way, p, slot, ss, rs).start()
        yield

    def gather_end(count, slot, ss, rs):
        for kind in (0, 2, 3):
            for p, way in kinds(kind, count):
                ag_copy(kind, way, p, slot, ss, rs).wait_recv()

    def gather_sent(count, slot, ss, rs):
        for kind in range(4):
            for p, way in kinds(kind, count):
                ag_copy(kind, way, p, slot, ss, rs).wait_send()

    def rs_copy(kind, way, p, own, stage, recv, ss, rs):
        sg = sign[way]
        src = stage.at[way, p] if kind == 3 else own(away(sg * (3, 4, 1)[kind]), p)
        to = away(sg * (1, 2, 1, 2)[kind])
        return remote(src, recv.at[kind, way, p], ss.at[kind, way, p], rs.at[kind, way, p], (s, to))

    def rs_kinds(kind, count):
        for p in range(count):
            for way in range(2):
                if kind != 1 or p % 2 == way:
                    yield p, way

    def scatter(count, own, stage, recv, ss, rs):
        for kind in (1, 0, 2):
            for p, way in rs_kinds(kind, count):
                rs_copy(kind, way, p, own, stage, recv, ss, rs).start()
        yield
        for p, way in rs_kinds(0, count):
            rs_copy(0, way, p, own, stage, recv, ss, rs).wait_recv()
            v = own(away(2 * sign[way]), p)[...].astype(F32) + recv[0, way, p].astype(F32)
            if p % 2 == way:
                rs_copy(1, way, p, own, stage, recv, ss, rs).wait_recv()
                v = v + recv[1, way, p].astype(F32)
            stage[way, p] = v.astype(BF)
            rs_copy(3, way, p, own, stage, recv, ss, rs).start()
        yield

    def scatter_end(p, own, stage, recv, ss, rs):
        v = own(g, p)[...].astype(F32)
        for kind in (2, 3):
            for way in range(2):
                rs_copy(kind, way, p, own, stage, recv, ss, rs).wait_recv()
                v = v + recv[kind, way, p].astype(F32)
        return v

    def scatter_sent(count, own, stage, recv, ss, rs):
        for kind in range(4):
            for p, way in rs_kinds(kind, count):
                rs_copy(kind, way, p, own, stage, recv, ss, rs).wait_send()

    loads[6].wait()

    def spread(i, c):
        at = pl.ds(pl.multiple_of(i * 128, 128), 128)
        row = jnp.broadcast_to(dsc_v[0:1, at], (128, 128))
        dcol[at, :] = row.T
        return c

    lax.fori_loop(0, NL // 128, spread, 0)
    loads[0].wait()

    def weigh(i, c):
        at = pl.ds(pl.multiple_of(i * 128, 128), 128)
        d = dcol[at, :]
        for n in range(NR // 128):
            cols = slice(n * 128, n * 128 + 128)
            wgt[at, cols] = (res[at, cols] * d).astype(BF)
        return c

    lax.fori_loop(0, NL // 128, weigh, 0)

    for n in (7, 8, 9):
        loads[n].wait()

    def name_blocks(j, x):
        at = jnp.int32(0)
        has = jnp.int32(0)
        for k in range(NCB):
            hit = jnp.where(bidx_s[0, k] == j, jnp.where(cnt_s[0, 0] > k, 1, 0), 0)
            at = jnp.where(hit == 1, k, at)
            has = jnp.where(hit == 1, 1, has)
        ctab[0, j] = at
        ctab[1, j] = has
        return x

    lax.fori_loop(0, NB2, name_blocks, 0)

    loads[1].wait()
    for k in range(NCB):
        v = dot_t(cbas[:, k * CB : (k + 1) * CB], wgt[...])
        crs[2 * k : 2 * k + 2] = v.astype(BF).reshape(2, HB, NR)

    def place(j, x):
        at = ctab[0, j] * 2
        has = ctab[1, j].astype(F32)
        for low in range(2):
            v = (crs[at + low].astype(F32) * has).astype(BF)
            for c in range(NCH):
                own[c, 2 * j + low] = v[:, c * W : (c + 1) * W]
        return x

    lax.fori_loop(0, NB2, place, 0)
    pl.semaphore_wait(bar, NG - 1 + NS - 1)

    def b_all(c):
        return (
            lambda d, p: own.at[c, d * NH + p],
            b_stage.at[c], b_recv.at[c], b_ss.at[c], b_rs.at[c],
        )

    def a_all(c):
        return NH, lambda o, p: rhs2.at[c, o * NH + p], a_ss.at[c], a_rs.at[c]

    def local_tile(i):
        def work():
            if i == 0:
                loads[2].wait()
            local[i * 256 : (i + 1) * 256, :] = dot(linv[i * 256 : (i + 1) * 256, :], wgt[...])

        return work

    def name_slots():
        def f(b, c):
            at = jnp.int32(0)
            has = jnp.int32(0)
            for j in range(MB2):
                hit = gidx_s[0, j] == b
                at = jnp.where(hit, j, at)
                has = jnp.where(hit, 1, has)
            gtab[0, b] = at
            gtab[1, b] = has
            return c

        lax.fori_loop(0, NB3, f, 0)

    def fill_perm(lo, hi):
        def f(b, c):
            k = lax.broadcasted_iota(jnp.int32, (128, 1024), 0)
            n = lax.broadcasted_iota(jnp.int32, (128, 1024), 1)
            want = (k // SL) * 128 + b * SL + k % SL
            at = pl.ds(pl.multiple_of(b * 128, 128), 128)
            perm[at, :] = jnp.where(n == want, 1.0, 0.0).astype(BF)
            return c

        return lambda: lax.fori_loop(lo, hi, f, 0)

    def retile():
        loads[5].wait()
        for q in range(4):
            tstage[q * SL : (q + 1) * SL, :] = l3inv[:, q * 1024 : (q + 1) * 1024]
        moved = dot(tstage[...], perm[...]).astype(BF)
        for m in range(NG):
            for q in range(4):
                v = moved[q * SL : (q + 1) * SL, m * 128 : (m + 1) * 128]
                tsend[m, :, q * 128 : (q + 1) * 128] = v
        tile[g] = tsend[g]

    def t_make(t):
        return tsend.at[t], tile.at[g]

    work = iter([local_tile(i) for i in range(4)] + [
        name_slots, fill_perm(0, 4), fill_perm(4, 8), retile
    ])

    def phase_w(c):
        next(work)()

    b_steps = [scatter(NH, *b_all(c)) for c in range(NCH)]
    a_steps = [gather(*a_all(c)) for c in range(NCH)]

    def phase_b(c):
        next(b_steps[c])

    def phase_a(c):
        next(a_steps[c])

    def d_all(c):
        return (
            lambda d, p: part.at[c, pl.ds(p * PJ, PJ), d],
            d_stage.at[c], d_recv.at[c], d_ss.at[c], d_rs.at[c],
        )

    d_steps = [scatter(MB2 // PJ, *d_all(c)) for c in range(NCH)]

    def phase_d(c):
        for q in range(NH):
            rhs2[c, g * NH + q] = scatter_end(q, *b_all(c)).astype(BF)
        if c == 0:
            loads[3].wait()
            loads[4].wait()
        mine = rhs2[c, pl.ds(g * NH, NH)].reshape(OWN2, W)
        for n in range(MB2 // 2):
            v = dot_t(l2bas[:, n * 256 : (n + 1) * 256], mine).astype(BF)
            part[c, 2 * n : 2 * n + 2] = v.reshape(2, NG, SL, W)
        next(d_steps[c])

    def phase_q(c):
        next(d_steps[c])

    def phase_s(c):
        gather_end(*a_all(c))
        l2loc[:, c * W : (c + 1) * W] = dot(l2inv[...], rhs2[c].reshape(NB2 * CB, W))

    def phase_t(c):
        start_all(z_copy, NG, t_make, t_ss, t_rs)

    def e_make(c):
        return lambda t: (dense.at[c, t], e_recv.at[c, s])

    def f_make(c):
        return lambda t: (xall.at[c, s], xall.at[c, s])

    def h_make(c):
        return lambda t: (hsend.at[c, t], h_recv.at[c, g])

    def i_make(c):
        return lambda t: (yall.at[c, s], yall.at[c, s])

    def j_all(c):
        return (
            MB2 // PJ, lambda o, p: lifted.at[c, pl.ds(p * PJ, PJ), o], j_ss.at[c], j_rs.at[c]
        )

    def l_all(c):
        return NH, lambda o, p: sol2.at[c, o * NH + p], l_ss.at[c], l_rs.at[c]

    j_steps = [gather(*j_all(c)) for c in range(NCH)]
    l_steps = [gather(*l_all(c)) for c in range(NCH)]

    def phase_t(c):
        start_all(z_copy, NG, t_make, t_ss, t_rs)

    def e_make(c):
        return lambda t: (dense.at[c, t], e_recv.at[c, s])

    def f_make(c):
        return lambda t: (xall.at[c, s], xall.at[c, s])

    def h_make(c):
        return lambda t: (hsend.at[c, t], h_recv.at[c, g])

    def i_make(c):
        return lambda t: (yall.at[c, s], yall.at[c, s])

    def j_make(c):
        return lambda t: (picked.at[c], lifted.at[c, :, g])

    def l_slot(c):
        return lambda o, q: sol2.at[c, o * NH + q]

    def phase_e(c):
        for p in range(MB2 // PJ):
            ssum[c, p * PJ : (p + 1) * PJ] = scatter_end(p, *d_all(c))

        def f(b, x):
            dense[c, b] = (ssum[c, gtab[0, b]] * gtab[1, b].astype(F32)).astype(BF)
            return x

        lax.fori_loop(0, NB3, f, 0)
        start_all(p_copy, NS, e_make(c), e_ss.at[c], e_rs.at[c])
        e_recv[c, s] = dense[c, s]

    def phase_f(c):
        recv_all(p_copy, NS, e_make(c), e_ss.at[c], e_rs.at[c])

        def f(b, v):
            return v + e_recv[c, b].astype(F32)

        xall[c, s] = lax.fori_loop(0, NS, f, jnp.zeros((SL, W), F32)).astype(BF)
        start_all(p_copy, NS, f_make(c), f_ss.at[c], f_rs.at[c])

    def phase_h(c):
        if c == 0:
            recv_all(z_copy, NG, t_make, t_ss, t_rs)
        recv_all(p_copy, NS, f_make(c), f_ss.at[c], f_rs.at[c])
        v = dot(tile[...].reshape(CB, NB3 * SL), xall[c].reshape(NB3 * SL, W))
        hsend[c] = v.astype(BF).reshape(NG, SL, W)
        start_all(z_copy, NG, h_make(c), h_ss.at[c], h_rs.at[c])
        h_recv[c, g] = hsend[c, g]

    def phase_i(c):
        recv_all(z_copy, NG, h_make(c), h_ss.at[c], h_rs.at[c])
        v = h_recv[c, 0].astype(F32)
        for m in range(1, NG):
            v = v + h_recv[c, m].astype(F32)
        yall[c, s] = v.astype(BF)
        start_all(p_copy, NS, i_make(c), i_ss.at[c], i_rs.at[c])

    def phase_j(c):
        recv_all(p_copy, NS, i_make(c), i_ss.at[c], i_rs.at[c])
        for j in range(MB2):
            lifted[c, j, g] = yall[c, gidx_s[0, j]]
        next(j_steps[c])

    def phase_g(c):
        next(j_steps[c])

    def phase_k(c):
        gather_end(*j_all(c))
        cols = slice(c * W, (c + 1) * W)
        v = l2loc[:, cols] + dot(l2bas[...], lifted[c].reshape(MB2 * CB, W))
        sol2[c, pl.ds(g * NH, NH)] = v.astype(BF).reshape(NH, HB, W)

    def phase_l(c):
        next(l_steps[c])

    def n_copy(c, f):
        dev = (
            (s, lax.rem(g + NG - 1, NG)),
            (s, lax.rem(g + 1, NG)),
            (lax.rem(s + NS - 1, NS), g),
            (lax.rem(s + 1, NS), g),
        )[f]
        return remote(fsend.at[c, f], f_recv.at[c, f ^ 1], n_ss.at[c, f], n_rs.at[c, f ^ 1], dev)

    def total_rows(c, lo, n):
        v = dot(cbas[lo : lo + n, :], chosen[c])
        cols = slice(c * W, (c + 1) * W)
        v = v + local[lo : lo + n, cols]
        d = dcol[lo : lo + n, :]
        if W > 128:
            d = jnp.concatenate([d] * (W // 128), axis=1)
        return v * d

    def phase_n(c):
        gather_end(*l_all(c))
        for k in range(NCB):
            for low in range(2):
                v = sol2[c, bidx_s[0, k] * 2 + low].astype(F32) * (cnt_s[0, 0] > k).astype(F32)
                at = k * CB + low * HB
                chosen[c, at : at + HB, :] = v.astype(BF)
        cols = slice(c * W, (c + 1) * W)
        for f in range(4):
            v = total_rows(c, f * CB, CB)
            out_ref[f * CB : (f + 1) * CB, cols] = v
            fsend[c, f] = v.astype(BF)
            n_copy(c, f).start()

    def phase_r(c):
        cols = slice(c * W, (c + 1) * W)
        for f in range(2, 4):
            out_ref[f * 256 : (f + 1) * 256, cols] = total_rows(c, f * 256, 256)

    def phase_o(c):
        cols = slice(c * W, (c + 1) * W)
        inside = (g > 0, g < NG - 1, s > 0, s < NS - 1)
        for f in range(4):
            n_copy(c, f ^ 1).wait_recv()
            at = slice(f * CB, (f + 1) * CB)
            v = f_recv[c, f].astype(F32) * inside[f].astype(F32)
            out_ref[at, cols] = out_ref[at, cols] + v

    phases = dict(
        a=phase_a, b=phase_b, w=phase_w, d=phase_d, s=phase_s, e=phase_e, f=phase_f, h=phase_h, i=phase_i,
        j=phase_j, g=phase_g, q=phase_q, t=phase_t, k=phase_k, l=phase_l, n=phase_n, r=phase_r, o=phase_o,
    )
    for name in ORDER:
        phases[name[0]](int(name[1]))

    sent_all(z_copy, NG, t_make, t_ss, t_rs)
    for c in range(NCH):
        scatter_sent(NH, *b_all(c))
        gather_sent(*a_all(c))
        scatter_sent(MB2 // PJ, *d_all(c))
        sent_all(p_copy, NS, e_make(c), e_ss.at[c], e_rs.at[c])
        sent_all(p_copy, NS, f_make(c), f_ss.at[c], f_rs.at[c])
        sent_all(z_copy, NG, h_make(c), h_ss.at[c], h_rs.at[c])
        sent_all(p_copy, NS, i_make(c), i_ss.at[c], i_rs.at[c])
        gather_sent(*j_all(c))
        gather_sent(*l_all(c))
        for f in range(4):
            n_copy(c, f).wait_send()


def local(
    residual,
    dscale,
    local_inverse,
    coarse_basis,
    block_counts,
    block_index,
    level2_inverse,
    level2_basis,
    group_index,
    level3_inverse,
):
    vm = pltpu.VMEM
    dma = pltpu.SemaphoreType.DMA
    vmem = pl.BlockSpec(memory_space=pltpu.VMEM)
    hbm = pl.BlockSpec(memory_space=pltpu.HBM)
    ring_sem = dma((NCH, 4, 2, NH))
    piece_sem = dma((NCH, 4, 2, MB2 // PJ))
    z_sem = dma((NCH, NG))
    p_sem = dma((NCH, NS))
    scratch = [
        pltpu.SMEM((1, 1), jnp.int32), pltpu.SMEM((1, NCB), jnp.int32), pltpu.SMEM((1, MB2), jnp.int32),
        vm((1, NL), F32), vm((NL, NR), F32), vm((NL, NL), BF), vm((NL, NCB * CB), BF), vm((OWN2, NB2 * CB), BF),
        vm((OWN2, MB2 * CB), BF), vm((SL, NB3 * CB), BF), dma((10,)),
        vm((NL, 128), F32), vm((NL, NR), BF), vm((NL, NR), F32), vm((1024, 1024), BF),
        vm((4 * SL, 1024), BF), vm((NG, SL, NB3 * SL), BF), vm((NG, SL, NB3 * SL), BF),
        dma((NG,)), dma((NG,)),
        pltpu.SMEM((2, NB2), jnp.int32), pltpu.SMEM((2, NB3), jnp.int32),
        vm((2 * NCB, HB, NR), BF), vm((NCH, NG * NH, HB, W), BF), vm((NCH, 2, NH, HB, W), BF),
        vm((NCH, 4, 2, NH, HB, W), BF), ring_sem, ring_sem,
        vm((NCH, NG * NH, HB, W), BF), ring_sem, ring_sem, vm((OWN2, NR), F32), vm((NCH, MB2, NG, SL, W), BF),
        vm((NCH, 2, MB2 // PJ, PJ, SL, W), BF), vm((NCH, 4, 2, MB2 // PJ, PJ, SL, W), BF), piece_sem, piece_sem,
        vm((NCH, MB2, SL, W), F32), vm((NCH, NB3, SL, W), BF), vm((NCH, NS, SL, W), BF), p_sem, p_sem,
        vm((NCH, NB3, SL, W), BF), p_sem, p_sem,
        vm((NCH, NG, SL, W), BF), vm((NCH, NG, SL, W), BF), z_sem, z_sem,
        vm((NCH, NB3, SL, W), BF), p_sem, p_sem,
        vm((NCH, MB2, NG, SL, W), BF), piece_sem, piece_sem,
        vm((NCH, NG * NH, HB, W), BF), ring_sem, ring_sem,
        vm((NCH, NCB * CB, W), BF), vm((NCH, 4, CB, W), BF), vm((NCH, 4, CB, W), BF),
        dma((NCH, 4)), dma((NCH, 4)),
    ]
    out = pl.pallas_call(
        kernel,
        out_shape=jax.ShapeDtypeStruct((NL, NR), F32),
        in_specs=[hbm] * 10,
        out_specs=vmem,
        scratch_shapes=scratch,
        name="bddc",
        compiler_params=pltpu.CompilerParams(
            collective_id=0, has_side_effects=True, vmem_limit_bytes=60 << 20
        ),
    )(
        block_counts.reshape(1, 1), block_index, group_index, dscale, residual[0], local_inverse[0],
        coarse_basis[0], level2_inverse[0], level2_basis[0], level3_inverse,
    )
    return out[None]


def solution(mesh):
    return jax.shard_map(
        local,
        mesh=mesh,
        in_specs=(
            P(("sub", "grp"), None, None),
            P(("sub", "grp"), None),
            P(("sub", "grp"), None, None),
            P(("sub", "grp"), None, None),
            P(("sub", "grp")),
            P(("sub", "grp"), None),
            P("sub", "grp", None),
            P("sub", "grp", None),
            P("sub", None),
            P(("sub", "grp"), None),
        ),
        out_specs=P(("sub", "grp"), None, None),
        check_vma=False,
    )
```

```python
import functools

import jax
import jax.numpy as jnp
from jax import lax
from jax.experimental import pallas as pl
from jax.experimental.pallas import tpu as pltpu
from jax.sharding import PartitionSpec as P

NS = 32
NG = 8
NL = 1024
NR = 256
CB = 128
NCB = 3
NB2 = 12
MB2 = 8
NB3 = 32
SL = CB // NG
OWN2 = NB2 * CB // NG
QB = 2
HB = CB // QB
NH = OWN2 // HB
NCH = 1
W = NR // NCH
PJ = 2

ORDER = (
    "b0", "w0", "w0", "w0", "w0", "w0", "b0", "w0", "w0", "w0", "d0", "q0", "e0", "t0", "a0", "f0", "a0",
    "h0", "i0", "j0", "s0", "g0", "x0", "k0", "l0", "y0", "l0", "n0", "r0", "o0",
)

MESH = pl.DeviceIdType.MESH
BF = jnp.bfloat16
F32 = jnp.float32


def dot(a, b):
    return jnp.dot(a, b, preferred_element_type=F32)


def dot_t(a, b):
    return lax.dot_general(a, b, (((0,), (0,)), ((), ())), preferred_element_type=F32)


def kernel(
    cnt_h, bidx_h, gidx_h, dsc_h, res_h, linv_h, cbas_h, l2inv_h, l2bas_h, l3inv_h,
    out_ref,
    cnt_s, bidx_s, gidx_s, dsc_v, res, linv, cbas, l2inv, l2bas, l3inv, load_sem,
    dcol, wgt, local, perm, tstage, tsend, tile, t_ss, t_rs,
    ctab, gtab,
    crs, own, b_stage, b_recv, b_ss, b_rs,
    rhs2, a_ss, a_rs, l2loc, part, d_stage, d_recv, d_ss, d_rs,
    ssum, dense, e_recv, e_ss, e_rs,
    xall, f_ss, f_rs,
    hsend, h_recv, h_ss, h_rs,
    yall, i_ss, i_rs,
    lifted, j_ss, j_rs,
    sol2, l_ss, l_rs,
    chosen, fsend, f_recv, n_ss, n_rs,
):
    s, g = lax.axis_index("sub"), lax.axis_index("grp")

    loads = [
        pltpu.make_async_copy(src, dst, load_sem.at[n])
        for n, (src, dst) in enumerate(
            [(res_h, res), (cbas_h, cbas), (linv_h, linv), (l2bas_h, l2bas), (l2inv_h, l2inv),
             (l3inv_h, l3inv), (dsc_h, dsc_v), (cnt_h, cnt_s), (bidx_h, bidx_s), (gidx_h, gidx_s)]
        )
    ]
    for n in (6, 0, 1, 7, 8, 9):
        loads[n].start()

    bar = pltpu.get_barrier_semaphore()

    def hail_z(i, c):
        pl.semaphore_signal(bar, inc=1, device_id=(s, lax.rem(g + i, NG)), device_id_type=MESH)
        return c

    def hail_p(i, c):
        pl.semaphore_signal(bar, inc=1, device_id=(lax.rem(s + i, NS), g), device_id_type=MESH)
        return c

    lax.fori_loop(1, NG, hail_z, 0)
    lax.fori_loop(1, NS, hail_p, 0)

    def remote(src, dst, ss, rs, dev):
        return pltpu.make_async_remote_copy(
            src_ref=src, dst_ref=dst, send_sem=ss, recv_sem=rs, device_id=dev, device_id_type=MESH
        )

    def z_start(make, ss, rs):
        def f(i, c):
            t = lax.rem(g + i, NG)
            src, dst = make(t)
            remote(src, dst, ss, rs, (s, t)).start()
            return c

        lax.fori_loop(1, NG, f, 0)

    def p_start(make, ss, rs):
        def f(i, c):
            t = lax.rem(s + i, NS)
            src, dst = make(t)
            remote(src, dst, ss, rs, (t, g)).start()
            return c

        lax.fori_loop(1, NS, f, 0)

    def all_of(some, ss, rs):
        return remote(some, some, ss, rs, (s, lax.rem(g + 1, NG)))

    sign = (1, -1)

    def away(n):
        return lax.rem(g + n + NG, NG)

    def kinds(kind, count):
        for p in range(count):
            for way in range(2):
                if kind != 3 or p % 2 == way:
                    yield p, way

    def ag_copy(kind, way, p, slot, ss, rs):
        o = g if kind < 2 else away(-2 * sign[way])
        ref = slot(o, p)
        to = away(sign[way] * (1, 2, 1, 2)[kind])
        return remote(ref, ref, ss.at[kind, way, p], rs.at[kind, way, p], (s, to))

    def gather(count, slot, ss, rs):
        for kind in (1, 0):
            for p, way in kinds(kind, count):
                ag_copy(kind, way, p, slot, ss, rs).start()
        yield
        for p, way in kinds(1, count):
            ag_copy(1, way, p, slot, ss, rs).wait_recv()
            ag_copy(2, way, p, slot, ss, rs).start()
            if p % 2 == way:
                ag_copy(3, way, p, slot, ss, rs).start()
        yield

    def gather_end(count, slot, ss, rs):
        for kind in (0, 2, 3):
            for p, way in kinds(kind, count):
                ag_copy(kind, way, p, slot, ss, rs).wait_recv()

    def gather_sent(count, slot, ss, rs):
        for kind in range(4):
            for p, way in kinds(kind, count):
                ag_copy(kind, way, p, slot, ss, rs).wait_send()

    def rs_copy(kind, way, p, own, stage, recv, ss, rs):
        sg = sign[way]
        src = stage.at[way, p] if kind == 3 else own(away(sg * (3, 4, 1)[kind]), p)
        to = away(sg * (1, 2, 1, 2)[kind])
        return remote(src, recv.at[kind, way, p], ss.at[kind, way, p], rs.at[kind, way, p], (s, to))

    def rs_kinds(kind, count):
        for p in range(count):
            for way in range(2):
                if kind != 1 or p % 2 == way:
                    yield p, way

    def scatter(count, own, stage, recv, ss, rs):
        for kind in (1, 0, 2):
            for p, way in rs_kinds(kind, count):
                rs_copy(kind, way, p, own, stage, recv, ss, rs).start()
        yield
        for p, way in rs_kinds(0, count):
            rs_copy(0, way, p, own, stage, recv, ss, rs).wait_recv()
            v = own(away(2 * sign[way]), p)[...].astype(F32) + recv[0, way, p].astype(F32)
            if p % 2 == way:
                rs_copy(1, way, p, own, stage, recv, ss, rs).wait_recv()
                v = v + recv[1, way, p].astype(F32)
            stage[way, p] = v.astype(BF)
            rs_copy(3, way, p, own, stage, recv, ss, rs).start()
        yield

    def scatter_end(p, own, stage, recv, ss, rs):
        v = own(g, p)[...].astype(F32)
        for kind in (2, 3):
            for way in range(2):
                rs_copy(kind, way, p, own, stage, recv, ss, rs).wait_recv()
                v = v + recv[kind, way, p].astype(F32)
        return v

    def scatter_sent(count, own, stage, recv, ss, rs):
        for kind in range(4):
            for p, way in rs_kinds(kind, count):
                rs_copy(kind, way, p, own, stage, recv, ss, rs).wait_send()

    loads[6].wait()

    def spread(i, c):
        at = pl.ds(pl.multiple_of(i * 128, 128), 128)
        row = jnp.broadcast_to(dsc_v[0:1, at], (128, 128))
        dcol[at, :] = row.T
        return c

    lax.fori_loop(0, NL // 128, spread, 0)
    loads[0].wait()

    def weigh(i, c):
        at = pl.ds(pl.multiple_of(i * 128, 128), 128)
        d = dcol[at, :]
        for n in range(NR // 128):
            cols = slice(n * 128, n * 128 + 128)
            wgt[at, cols] = (res[at, cols] * d).astype(BF)
        return c

    lax.fori_loop(0, NL // 128, weigh, 0)

    for n in (2, 3, 4, 5):
        loads[n].start()

    for n in (7, 8, 9):
        loads[n].wait()

    def name_blocks(j, x):
        at = jnp.int32(0)
        has = jnp.int32(0)
        for k in range(NCB):
            hit = jnp.where(bidx_s[0, k] == j, jnp.where(cnt_s[0, 0] > k, 1, 0), 0)
            at = jnp.where(hit == 1, k, at)
            has = jnp.where(hit == 1, 1, has)
        ctab[0, j] = at
        ctab[1, j] = has
        return x

    lax.fori_loop(0, NB2, name_blocks, 0)

    loads[1].wait()
    for k in range(NCB):
        v = dot_t(cbas[:, k * CB : (k + 1) * CB], wgt[...])
        crs[QB * k : QB * k + QB] = v.astype(BF).reshape(QB, HB, NR)

    def place(j, x):
        at = ctab[0, j] * QB
        has = ctab[1, j].astype(F32)
        for low in range(QB):
            v = (crs[at + low].astype(F32) * has).astype(BF)
            for c in range(NCH):
                own[c, QB * j + low] = v[:, c * W : (c + 1) * W]
        return x

    lax.fori_loop(0, NB2, place, 0)
    pl.semaphore_wait(bar, NG - 1 + NS - 1)

    def b_all(c):
        return (
            lambda d, p: own.at[c, d * NH + p],
            b_stage.at[c], b_recv.at[c], b_ss.at[c], b_rs.at[c],
        )

    def a_all(c):
        return NH, lambda o, p: rhs2.at[c, o * NH + p], a_ss.at[c], a_rs.at[c]

    def local_tile(i):
        def work():
            if i == 0:
                loads[2].wait()
            local[i * 256 : (i + 1) * 256, :] = dot(linv[i * 256 : (i + 1) * 256, :], wgt[...])

        return work

    def name_slots():
        def f(b, c):
            at = jnp.int32(0)
            has = jnp.int32(0)
            for j in range(MB2):
                hit = gidx_s[0, j] == b
                at = jnp.where(hit, j, at)
                has = jnp.where(hit, 1, has)
            gtab[0, b] = at
            gtab[1, b] = has
            return c

        lax.fori_loop(0, NB3, f, 0)

    def fill_perm(lo, hi):
        def f(b, c):
            k = lax.broadcasted_iota(jnp.int32, (128, 1024), 0)
            n = lax.broadcasted_iota(jnp.int32, (128, 1024), 1)
            want = (k // SL) * 128 + b * SL + k % SL
            at = pl.ds(pl.multiple_of(b * 128, 128), 128)
            perm[at, :] = jnp.where(n == want, 1.0, 0.0).astype(BF)
            return c

        return lambda: lax.fori_loop(lo, hi, f, 0)

    def retile():
        loads[5].wait()
        for q in range(4):
            tstage[q * SL : (q + 1) * SL, :] = l3inv[:, q * 1024 : (q + 1) * 1024]
        moved = dot(tstage[...], perm[...]).astype(BF)
        for m in range(NG):
            for q in range(4):
                v = moved[q * SL : (q + 1) * SL, m * 128 : (m + 1) * 128]
                tsend[m, :, q * 128 : (q + 1) * 128] = v
        tile[g] = tsend[g]

    def t_make(t):
        return tsend.at[t], tile.at[g]

    work = iter([local_tile(i) for i in range(4)] + [
        name_slots, fill_perm(0, 4), fill_perm(4, 8), retile
    ])

    def phase_w(c):
        next(work)()

    b_steps = [scatter(NH, *b_all(c)) for c in range(NCH)]
    a_steps = [gather(*a_all(c)) for c in range(NCH)]

    def phase_b(c):
        next(b_steps[c])

    def phase_a(c):
        next(a_steps[c])

    def d_all(c):
        return (
            lambda d, p: part.at[c, pl.ds(p * PJ, PJ), d],
            d_stage.at[c], d_recv.at[c], d_ss.at[c], d_rs.at[c],
        )

    d_steps = [scatter(MB2 // PJ, *d_all(c)) for c in range(NCH)]

    def phase_d(c):
        for q in range(NH):
            rhs2[c, g * NH + q] = scatter_end(q, *b_all(c)).astype(BF)
        if c == 0:
            loads[3].wait()
            loads[4].wait()
        mine = rhs2[c, pl.ds(g * NH, NH)].reshape(OWN2, W)
        for n in range(MB2 // 2):
            v = dot_t(l2bas[:, n * 256 : (n + 1) * 256], mine).astype(BF)
            part[c, 2 * n : 2 * n + 2] = v.reshape(2, NG, SL, W)
        next(d_steps[c])

    def phase_q(c):
        next(d_steps[c])

    def phase_s(c):
        gather_end(*a_all(c))
        l2loc[:, c * W : (c + 1) * W] = dot(l2inv[...], rhs2[c].reshape(NB2 * CB, W))

    def e_make(c):
        return lambda t: (dense.at[c, t], e_recv.at[c, s])

    def f_make(c):
        return lambda t: (xall.at[c, s], xall.at[c, s])

    def h_make(c):
        return lambda t: (hsend.at[c, t], h_recv.at[c, g])

    def i_make(c):
        return lambda t: (yall.at[c, s], yall.at[c, s])

    def e_all(c):
        return all_of(e_recv.at[c, pl.ds(1, NS - 1)], e_ss.at[c], e_rs.at[c])

    def f_all(c):
        return all_of(xall.at[c, pl.ds(1, NS - 1)], f_ss.at[c], f_rs.at[c])

    def i_all(c):
        return all_of(yall.at[c, pl.ds(1, NS - 1)], i_ss.at[c], i_rs.at[c])

    def h_all(c):
        return all_of(h_recv.at[c, pl.ds(1, NG - 1)], h_ss.at[c], h_rs.at[c])

    def t_all():
        return all_of(tile.at[pl.ds(1, NG - 1)], t_ss, t_rs)

    def j_all(c):
        return (
            MB2 // PJ, lambda o, p: lifted.at[c, pl.ds(p * PJ, PJ), o], j_ss.at[c], j_rs.at[c]
        )

    def l_all(c):
        return NH, lambda o, p: sol2.at[c, o * NH + p], l_ss.at[c], l_rs.at[c]

    j_steps = [gather(*j_all(c)) for c in range(NCH)]
    l_steps = [gather(*l_all(c)) for c in range(NCH)]

    def phase_t(c):
        z_start(t_make, t_ss, t_rs)

    def e_make(c):
        return lambda t: (dense.at[c, t], e_recv.at[c, s])

    def f_make(c):
        return lambda t: (xall.at[c, s], xall.at[c, s])

    def h_make(c):
        return lambda t: (hsend.at[c, t], h_recv.at[c, g])

    def i_make(c):
        return lambda t: (yall.at[c, s], yall.at[c, s])

    def j_make(c):
        return lambda t: (picked.at[c], lifted.at[c, :, g])

    def l_slot(c):
        return lambda o, q: sol2.at[c, o * NH + q]

    def phase_e(c):
        for p in range(MB2 // PJ):
            ssum[c, p * PJ : (p + 1) * PJ] = scatter_end(p, *d_all(c))

        def f(b, x):
            dense[c, b] = (ssum[c, gtab[0, b]] * gtab[1, b].astype(F32)).astype(BF)
            return x

        lax.fori_loop(0, NB3, f, 0)
        p_start(e_make(c), e_ss.at[c], e_rs.at[c])
        e_recv[c, s] = dense[c, s]

    def phase_f(c):
        e_all(c).wait_recv()

        def f(b, v):
            return v + e_recv[c, b].astype(F32)

        xall[c, s] = lax.fori_loop(0, NS, f, jnp.zeros((SL, W), F32)).astype(BF)
        p_start(f_make(c), f_ss.at[c], f_rs.at[c])

    def phase_h(c):
        if c == 0:
            t_all().wait_recv()
        f_all(c).wait_recv()
        v = dot(tile[...].reshape(CB, NB3 * SL), xall[c].reshape(NB3 * SL, W))
        hsend[c] = v.astype(BF).reshape(NG, SL, W)
        z_start(h_make(c), h_ss.at[c], h_rs.at[c])
        h_recv[c, g] = hsend[c, g]

    def phase_i(c):
        h_all(c).wait_recv()
        v = h_recv[c, 0].astype(F32)
        for m in range(1, NG):
            v = v + h_recv[c, m].astype(F32)
        yall[c, s] = v.astype(BF)
        p_start(i_make(c), i_ss.at[c], i_rs.at[c])

    def phase_j(c):
        i_all(c).wait_recv()
        for j in range(MB2):
            lifted[c, j, g] = yall[c, gidx_s[0, j]]
        next(j_steps[c])

    def phase_g(c):
        next(j_steps[c])

    def phase_k(c):
        gather_end(*j_all(c))
        cols = slice(c * W, (c + 1) * W)
        v = l2loc[:, cols] + dot(l2bas[...], lifted[c].reshape(MB2 * CB, W))
        sol2[c, pl.ds(g * NH, NH)] = v.astype(BF).reshape(NH, HB, W)

    def phase_l(c):
        next(l_steps[c])

    def phase_x(c):
        scatter_sent(NH, *b_all(c))
        scatter_sent(MB2 // PJ, *d_all(c))
        if c == 0:
            t_all().wait_send()
        for each in (e_all, f_all, h_all, i_all):
            each(c).wait_send()
        gather_sent(*a_all(c))

    def phase_y(c):
        gather_sent(*j_all(c))

    def n_copy(c, f):
        dev = (
            (s, lax.rem(g + NG - 1, NG)),
            (s, lax.rem(g + 1, NG)),
            (lax.rem(s + NS - 1, NS), g),
            (lax.rem(s + 1, NS), g),
        )[f]
        return remote(fsend.at[c, f], f_recv.at[c, f ^ 1], n_ss.at[c, f], n_rs.at[c, f ^ 1], dev)

    def total_rows(c, lo, n):
        v = dot(cbas[lo : lo + n, :], chosen[c])
        cols = slice(c * W, (c + 1) * W)
        v = v + local[lo : lo + n, cols]
        d = dcol[lo : lo + n, :]
        if W > 128:
            d = jnp.concatenate([d] * (W // 128), axis=1)
        return v * d

    def phase_n(c):
        gather_end(*l_all(c))
        for k in range(NCB):
            for low in range(QB):
                v = sol2[c, bidx_s[0, k] * QB + low].astype(F32) * (cnt_s[0, 0] > k).astype(F32)
                at = k * CB + low * HB
                chosen[c, at : at + HB, :] = v.astype(BF)
        cols = slice(c * W, (c + 1) * W)
        for f in range(4):
            v = total_rows(c, f * CB, CB)
            out_ref[f * CB : (f + 1) * CB, cols] = v
            fsend[c, f] = v.astype(BF)
            n_copy(c, f).start()

    def phase_r(c):
        cols = slice(c * W, (c + 1) * W)
        for f in range(2, 4):
            out_ref[f * 256 : (f + 1) * 256, cols] = total_rows(c, f * 256, 256)

    def phase_o(c):
        cols = slice(c * W, (c + 1) * W)
        inside = (g > 0, g < NG - 1, s > 0, s < NS - 1)
        for f in range(4):
            n_copy(c, f ^ 1).wait_recv()
            at = slice(f * CB, (f + 1) * CB)
            v = f_recv[c, f].astype(F32) * inside[f].astype(F32)
            out_ref[at, cols] = out_ref[at, cols] + v

    phases = dict(
        a=phase_a, b=phase_b, w=phase_w, d=phase_d, s=phase_s, e=phase_e, f=phase_f, h=phase_h, i=phase_i,
        j=phase_j, g=phase_g, q=phase_q, t=phase_t, x=phase_x, y=phase_y, k=phase_k, l=phase_l, n=phase_n, r=phase_r, o=phase_o,
    )
    for name in ORDER:
        phases[name[0]](int(name[1]))

    for c in range(NCH):
        gather_sent(*l_all(c))
        for f in range(4):
            n_copy(c, f).wait_send()


def local(
    residual,
    dscale,
    local_inverse,
    coarse_basis,
    block_counts,
    block_index,
    level2_inverse,
    level2_basis,
    group_index,
    level3_inverse,
):
    vm = pltpu.VMEM
    dma = pltpu.SemaphoreType.DMA
    vmem = pl.BlockSpec(memory_space=pltpu.VMEM)
    hbm = pl.BlockSpec(memory_space=pltpu.HBM)
    ring_sem = dma((NCH, 4, 2, NH))
    piece_sem = dma((NCH, 4, 2, MB2 // PJ))
    one_sem = dma((NCH,))
    scratch = [
        pltpu.SMEM((1, 1), jnp.int32), pltpu.SMEM((1, NCB), jnp.int32), pltpu.SMEM((1, MB2), jnp.int32),
        vm((1, NL), F32), vm((NL, NR), F32), vm((NL, NL), BF), vm((NL, NCB * CB), BF), vm((OWN2, NB2 * CB), BF),
        vm((OWN2, MB2 * CB), BF), vm((SL, NB3 * CB), BF), dma((10,)),
        vm((NL, 128), F32), vm((NL, NR), BF), vm((NL, NR), F32), vm((1024, 1024), BF),
        vm((4 * SL, 1024), BF), vm((NG, SL, NB3 * SL), BF), vm((NG, SL, NB3 * SL), BF),
        dma(()), dma(()),
        pltpu.SMEM((2, NB2), jnp.int32), pltpu.SMEM((2, NB3), jnp.int32),
        vm((QB * NCB, HB, NR), BF), vm((NCH, NG * NH, HB, W), BF), vm((NCH, 2, NH, HB, W), BF),
        vm((NCH, 4, 2, NH, HB, W), BF), ring_sem, ring_sem,
        vm((NCH, NG * NH, HB, W), BF), ring_sem, ring_sem, vm((OWN2, NR), F32), vm((NCH, MB2, NG, SL, W), BF),
        vm((NCH, 2, MB2 // PJ, PJ, SL, W), BF), vm((NCH, 4, 2, MB2 // PJ, PJ, SL, W), BF), piece_sem, piece_sem,
        vm((NCH, MB2, SL, W), F32), vm((NCH, NB3, SL, W), BF), vm((NCH, NS, SL, W), BF), one_sem, one_sem,
        vm((NCH, NB3, SL, W), BF), one_sem, one_sem,
        vm((NCH, NG, SL, W), BF), vm((NCH, NG, SL, W), BF), one_sem, one_sem,
        vm((NCH, NB3, SL, W), BF), one_sem, one_sem,
        vm((NCH, MB2, NG, SL, W), BF), piece_sem, piece_sem,
        vm((NCH, NG * NH, HB, W), BF), ring_sem, ring_sem,
        vm((NCH, NCB * CB, W), BF), vm((NCH, 4, CB, W), BF), vm((NCH, 4, CB, W), BF),
        dma((NCH, 4)), dma((NCH, 4)),
    ]
    out = pl.pallas_call(
        kernel,
        out_shape=jax.ShapeDtypeStruct((NL, NR), F32),
        in_specs=[hbm] * 10,
        out_specs=vmem,
        scratch_shapes=scratch,
        name="bddc",
        compiler_params=pltpu.CompilerParams(
            collective_id=0, has_side_effects=True, vmem_limit_bytes=60 << 20
        ),
    )(
        block_counts.reshape(1, 1), block_index, group_index, dscale, residual[0], local_inverse[0],
        coarse_basis[0], level2_inverse[0], level2_basis[0], level3_inverse,
    )
    return out[None]


def solution(mesh):
    return jax.shard_map(
        local,
        mesh=mesh,
        in_specs=(
            P(("sub", "grp"), None, None),
            P(("sub", "grp"), None),
            P(("sub", "grp"), None, None),
            P(("sub", "grp"), None, None),
            P(("sub", "grp")),
            P(("sub", "grp"), None),
            P("sub", "grp", None),
            P("sub", "grp", None),
            P("sub", None),
            P(("sub", "grp"), None),
        ),
        out_specs=P(("sub", "grp"), None, None),
        check_vma=False,
    )
```

```python
import functools

import jax
import jax.numpy as jnp
from jax import lax
from jax.experimental import pallas as pl
from jax.experimental.pallas import tpu as pltpu
from jax.sharding import PartitionSpec as P

NS = 32
NG = 8
NL = 1024
NR = 256
CB = 128
NCB = 3
NB2 = 12
MB2 = 8
NB3 = 32
SL = CB // NG
OWN2 = NB2 * CB // NG
QB = 4
HB = CB // QB
NH = OWN2 // HB
NCH = 1
W = NR // NCH
PJ = 2

ORDER = (
    "b0", "w0", "w0", "w0", "w0", "w0", "b0", "w0", "w0", "w0", "d0", "q0", "e0", "t0", "a0", "f0", "a0",
    "h0", "i0", "j0", "s0", "g0", "x0", "k0", "l0", "y0", "l0", "n0", "r0", "o0",
)

MESH = pl.DeviceIdType.MESH
BF = jnp.bfloat16
F32 = jnp.float32


def dot(a, b):
    return jnp.dot(a, b, preferred_element_type=F32)


def dot_t(a, b):
    return lax.dot_general(a, b, (((0,), (0,)), ((), ())), preferred_element_type=F32)


def kernel(
    cnt_h, bidx_h, gidx_h, dsc_h, res_h, linv_h, cbas_h, l2inv_h, l2bas_h, l3inv_h,
    out_ref,
    cnt_s, bidx_s, gidx_s, dsc_v, res, linv, cbas, l2inv, l2bas, l3inv, load_sem,
    dcol, wgt, local, perm, tstage, tsend, tile, t_ss, t_rs,
    ctab, gtab,
    crs, own, b_stage, b_recv, b_ss, b_rs,
    rhs2, a_ss, a_rs, l2loc, part, d_stage, d_recv, d_ss, d_rs,
    ssum, dense, e_recv, e_ss, e_rs,
    xall, f_ss, f_rs,
    hsend, h_recv, h_ss, h_rs,
    yall, i_ss, i_rs,
    lifted, j_ss, j_rs,
    sol2, l_ss, l_rs,
    chosen, fsend, f_recv, n_ss, n_rs,
):
    s, g = lax.axis_index("sub"), lax.axis_index("grp")

    loads = [
        pltpu.make_async_copy(src, dst, load_sem.at[n])
        for n, (src, dst) in enumerate(
            [(res_h, res), (cbas_h, cbas), (linv_h, linv), (l2bas_h, l2bas), (l2inv_h, l2inv),
             (l3inv_h, l3inv), (dsc_h, dsc_v), (cnt_h, cnt_s), (bidx_h, bidx_s), (gidx_h, gidx_s)]
        )
    ]
    for n in (6, 0, 1, 7, 8, 9):
        loads[n].start()

    bar = pltpu.get_barrier_semaphore()

    def hail_z(i, c):
        pl.semaphore_signal(bar, inc=1, device_id=(s, lax.rem(g + i, NG)), device_id_type=MESH)
        return c

    def hail_p(i, c):
        pl.semaphore_signal(bar, inc=1, device_id=(lax.rem(s + i, NS), g), device_id_type=MESH)
        return c

    lax.fori_loop(1, NG, hail_z, 0)
    lax.fori_loop(1, NS, hail_p, 0)

    def remote(src, dst, ss, rs, dev):
        return pltpu.make_async_remote_copy(
            src_ref=src, dst_ref=dst, send_sem=ss, recv_sem=rs, device_id=dev, device_id_type=MESH
        )

    def z_start(make, ss, rs):
        def f(i, c):
            t = lax.rem(g + i, NG)
            src, dst = make(t)
            remote(src, dst, ss, rs, (s, t)).start()
            return c

        lax.fori_loop(1, NG, f, 0)

    def p_start(make, ss, rs):
        def f(i, c):
            t = lax.rem(s + i, NS)
            src, dst = make(t)
            remote(src, dst, ss, rs, (t, g)).start()
            return c

        lax.fori_loop(1, NS, f, 0)

    def all_of(some, ss, rs):
        return remote(some, some, ss, rs, (s, lax.rem(g + 1, NG)))

    sign = (1, -1)

    def away(n):
        return lax.rem(g + n + NG, NG)

    def kinds(kind, count):
        for p in range(count):
            for way in range(2):
                if kind != 3 or p % 2 == way:
                    yield p, way

    def ag_copy(kind, way, p, slot, ss, rs):
        o = g if kind < 2 else away(-2 * sign[way])
        ref = slot(o, p)
        to = away(sign[way] * (1, 2, 1, 2)[kind])
        return remote(ref, ref, ss.at[kind, way, p], rs.at[kind, way, p], (s, to))

    def gather(count, slot, ss, rs):
        for kind in (1, 0):
            for p, way in kinds(kind, count):
                ag_copy(kind, way, p, slot, ss, rs).start()
        yield
        for p, way in kinds(1, count):
            ag_copy(1, way, p, slot, ss, rs).wait_recv()
            ag_copy(2, way, p, slot, ss, rs).start()
            if p % 2 == way:
                ag_copy(3, way, p, slot, ss, rs).start()
        yield

    def gather_end(count, slot, ss, rs):
        for kind in (0, 2, 3):
            for p, way in kinds(kind, count):
                ag_copy(kind, way, p, slot, ss, rs).wait_recv()

    def gather_sent(count, slot, ss, rs):
        for kind in range(4):
            for p, way in kinds(kind, count):
                ag_copy(kind, way, p, slot, ss, rs).wait_send()

    def rs_copy(kind, way, p, own, stage, recv, ss, rs):
        sg = sign[way]
        src = stage.at[way, p] if kind == 3 else own(away(sg * (3, 4, 1)[kind]), p)
        to = away(sg * (1, 2, 1, 2)[kind])
        return remote(src, recv.at[kind, way, p], ss.at[kind, way, p], rs.at[kind, way, p], (s, to))

    def rs_kinds(kind, count):
        for p in range(count):
            for way in range(2):
                if kind != 1 or p % 2 == way:
                    yield p, way

    def scatter(count, own, stage, recv, ss, rs):
        for kind in (1, 0, 2):
            for p, way in rs_kinds(kind, count):
                rs_copy(kind, way, p, own, stage, recv, ss, rs).start()
        yield
        for p, way in rs_kinds(0, count):
            rs_copy(0, way, p, own, stage, recv, ss, rs).wait_recv()
            v = own(away(2 * sign[way]), p)[...].astype(F32) + recv[0, way, p].astype(F32)
            if p % 2 == way:
                rs_copy(1, way, p, own, stage, recv, ss, rs).wait_recv()
                v = v + recv[1, way, p].astype(F32)
            stage[way, p] = v.astype(BF)
            rs_copy(3, way, p, own, stage, recv, ss, rs).start()
        yield

    def scatter_end(p, own, stage, recv, ss, rs):
        v = own(g, p)[...].astype(F32)
        for kind in (2, 3):
            for way in range(2):
                rs_copy(kind, way, p, own, stage, recv, ss, rs).wait_recv()
                v = v + recv[kind, way, p].astype(F32)
        return v

    def scatter_sent(count, own, stage, recv, ss, rs):
        for kind in range(4):
            for p, way in rs_kinds(kind, count):
                rs_copy(kind, way, p, own, stage, recv, ss, rs).wait_send()

    loads[6].wait()

    def spread(i, c):
        at = pl.ds(pl.multiple_of(i * 128, 128), 128)
        row = jnp.broadcast_to(dsc_v[0:1, at], (128, 128))
        dcol[at, :] = row.T
        return c

    lax.fori_loop(0, NL // 128, spread, 0)
    loads[0].wait()

    def weigh(i, c):
        at = pl.ds(pl.multiple_of(i * 128, 128), 128)
        d = dcol[at, :]
        for n in range(NR // 128):
            cols = slice(n * 128, n * 128 + 128)
            wgt[at, cols] = (res[at, cols] * d).astype(BF)
        return c

    lax.fori_loop(0, NL // 128, weigh, 0)

    for n in (2, 3, 4, 5):
        loads[n].start()

    for n in (7, 8, 9):
        loads[n].wait()

    def name_blocks(j, x):
        at = jnp.int32(0)
        has = jnp.int32(0)
        for k in range(NCB):
            hit = jnp.where(bidx_s[0, k] == j, jnp.where(cnt_s[0, 0] > k, 1, 0), 0)
            at = jnp.where(hit == 1, k, at)
            has = jnp.where(hit == 1, 1, has)
        ctab[0, j] = at
        ctab[1, j] = has
        return x

    lax.fori_loop(0, NB2, name_blocks, 0)

    loads[1].wait()
    for k in range(NCB):
        v = dot_t(cbas[:, k * CB : (k + 1) * CB], wgt[...])
        crs[QB * k : QB * k + QB] = v.astype(BF).reshape(QB, HB, NR)

    def place(j, x):
        at = ctab[0, j] * QB
        has = ctab[1, j].astype(F32)
        for low in range(QB):
            v = (crs[at + low].astype(F32) * has).astype(BF)
            for c in range(NCH):
                own[c, QB * j + low] = v[:, c * W : (c + 1) * W]
        return x

    lax.fori_loop(0, NB2, place, 0)
    pl.semaphore_wait(bar, NG - 1 + NS - 1)

    def b_all(c):
        return (
            lambda d, p: own.at[c, d * NH + p],
            b_stage.at[c], b_recv.at[c], b_ss.at[c], b_rs.at[c],
        )

    def a_all(c):
        return NH, lambda o, p: rhs2.at[c, o * NH + p], a_ss.at[c], a_rs.at[c]

    def local_tile(i):
        def work():
            if i == 0:
                loads[2].wait()
            local[i * 256 : (i + 1) * 256, :] = dot(linv[i * 256 : (i + 1) * 256, :], wgt[...])

        return work

    def name_slots():
        def f(b, c):
            at = jnp.int32(0)
            has = jnp.int32(0)
            for j in range(MB2):
                hit = gidx_s[0, j] == b
                at = jnp.where(hit, j, at)
                has = jnp.where(hit, 1, has)
            gtab[0, b] = at
            gtab[1, b] = has
            return c

        lax.fori_loop(0, NB3, f, 0)

    def fill_perm(lo, hi):
        def f(b, c):
            k = lax.broadcasted_iota(jnp.int32, (128, 1024), 0)
            n = lax.broadcasted_iota(jnp.int32, (128, 1024), 1)
            want = (k // SL) * 128 + b * SL + k % SL
            at = pl.ds(pl.multiple_of(b * 128, 128), 128)
            perm[at, :] = jnp.where(n == want, 1.0, 0.0).astype(BF)
            return c

        return lambda: lax.fori_loop(lo, hi, f, 0)

    def retile():
        loads[5].wait()
        for q in range(4):
            tstage[q * SL : (q + 1) * SL, :] = l3inv[:, q * 1024 : (q + 1) * 1024]
        moved = dot(tstage[...], perm[...]).astype(BF)
        for m in range(NG):
            for q in range(4):
                v = moved[q * SL : (q + 1) * SL, m * 128 : (m + 1) * 128]
                tsend[m, :, q * 128 : (q + 1) * 128] = v
        tile[g] = tsend[g]

    def t_make(t):
        return tsend.at[t], tile.at[g]

    work = iter([local_tile(i) for i in range(4)] + [
        name_slots, fill_perm(0, 4), fill_perm(4, 8), retile
    ])

    def phase_w(c):
        next(work)()

    b_steps = [scatter(NH, *b_all(c)) for c in range(NCH)]
    a_steps = [gather(*a_all(c)) for c in range(NCH)]

    def phase_b(c):
        next(b_steps[c])

    def phase_a(c):
        next(a_steps[c])

    def d_all(c):
        return (
            lambda d, p: part.at[c, pl.ds(p * PJ, PJ), d],
            d_stage.at[c], d_recv.at[c], d_ss.at[c], d_rs.at[c],
        )

    d_steps = [scatter(MB2 // PJ, *d_all(c)) for c in range(NCH)]

    def phase_d(c):
        for q in range(NH):
            rhs2[c, g * NH + q] = scatter_end(q, *b_all(c)).astype(BF)
        if c == 0:
            loads[3].wait()
            loads[4].wait()
        mine = rhs2[c, pl.ds(g * NH, NH)].reshape(OWN2, W)
        for n in range(MB2 // 2):
            v = dot_t(l2bas[:, n * 256 : (n + 1) * 256], mine).astype(BF)
            part[c, 2 * n : 2 * n + 2] = v.reshape(2, NG, SL, W)
        next(d_steps[c])

    def phase_q(c):
        next(d_steps[c])

    def phase_s(c):
        gather_end(*a_all(c))
        l2loc[:, c * W : (c + 1) * W] = dot(l2inv[...], rhs2[c].reshape(NB2 * CB, W))

    def e_make(c):
        return lambda t: (dense.at[c, t], e_recv.at[c, s])

    def f_make(c):
        return lambda t: (xall.at[c, s], xall.at[c, s])

    def h_make(c):
        return lambda t: (hsend.at[c, t], h_recv.at[c, g])

    def i_make(c):
        return lambda t: (yall.at[c, s], yall.at[c, s])

    def e_all(c):
        return all_of(e_recv.at[c, pl.ds(1, NS - 1)], e_ss.at[c], e_rs.at[c])

    def f_all(c):
        return all_of(xall.at[c, pl.ds(1, NS - 1)], f_ss.at[c], f_rs.at[c])

    def i_all(c):
        return all_of(yall.at[c, pl.ds(1, NS - 1)], i_ss.at[c], i_rs.at[c])

    def h_all(c):
        return all_of(h_recv.at[c, pl.ds(1, NG - 1)], h_ss.at[c], h_rs.at[c])

    def t_all():
        return all_of(tile.at[pl.ds(1, NG - 1)], t_ss, t_rs)

    def j_all(c):
        return (
            MB2 // PJ, lambda o, p: lifted.at[c, pl.ds(p * PJ, PJ), o], j_ss.at[c], j_rs.at[c]
        )

    def l_all(c):
        return NH, lambda o, p: sol2.at[c, o * NH + p], l_ss.at[c], l_rs.at[c]

    j_steps = [gather(*j_all(c)) for c in range(NCH)]
    l_steps = [gather(*l_all(c)) for c in range(NCH)]

    def phase_t(c):
        z_start(t_make, t_ss, t_rs)

    def e_make(c):
        return lambda t: (dense.at[c, t], e_recv.at[c, s])

    def f_make(c):
        return lambda t: (xall.at[c, s], xall.at[c, s])

    def h_make(c):
        return lambda t: (hsend.at[c, t], h_recv.at[c, g])

    def i_make(c):
        return lambda t: (yall.at[c, s], yall.at[c, s])

    def j_make(c):
        return lambda t: (picked.at[c], lifted.at[c, :, g])

    def l_slot(c):
        return lambda o, q: sol2.at[c, o * NH + q]

    def phase_e(c):
        for p in range(MB2 // PJ):
            ssum[c, p * PJ : (p + 1) * PJ] = scatter_end(p, *d_all(c))

        def f(b, x):
            dense[c, b] = (ssum[c, gtab[0, b]] * gtab[1, b].astype(F32)).astype(BF)
            return x

        lax.fori_loop(0, NB3, f, 0)
        p_start(e_make(c), e_ss.at[c], e_rs.at[c])
        e_recv[c, s] = dense[c, s]

    def phase_f(c):
        e_all(c).wait_recv()

        def f(b, v):
            return v + e_recv[c, b].astype(F32)

        xall[c, s] = lax.fori_loop(0, NS, f, jnp.zeros((SL, W), F32)).astype(BF)
        p_start(f_make(c), f_ss.at[c], f_rs.at[c])

    def phase_h(c):
        if c == 0:
            t_all().wait_recv()
        f_all(c).wait_recv()
        v = dot(tile[...].reshape(CB, NB3 * SL), xall[c].reshape(NB3 * SL, W))
        hsend[c] = v.astype(BF).reshape(NG, SL, W)
        z_start(h_make(c), h_ss.at[c], h_rs.at[c])
        h_recv[c, g] = hsend[c, g]

    def phase_i(c):
        h_all(c).wait_recv()
        v = h_recv[c, 0].astype(F32)
        for m in range(1, NG):
            v = v + h_recv[c, m].astype(F32)
        yall[c, s] = v.astype(BF)
        p_start(i_make(c), i_ss.at[c], i_rs.at[c])

    def phase_j(c):
        i_all(c).wait_recv()
        for j in range(MB2):
            lifted[c, j, g] = yall[c, gidx_s[0, j]]
        next(j_steps[c])

    def phase_g(c):
        next(j_steps[c])

    def phase_k(c):
        gather_end(*j_all(c))
        cols = slice(c * W, (c + 1) * W)
        v = l2loc[:, cols] + dot(l2bas[...], lifted[c].reshape(MB2 * CB, W))
        sol2[c, pl.ds(g * NH, NH)] = v.astype(BF).reshape(NH, HB, W)

    def phase_l(c):
        next(l_steps[c])

    def phase_x(c):
        scatter_sent(NH, *b_all(c))
        scatter_sent(MB2 // PJ, *d_all(c))
        if c == 0:
            t_all().wait_send()
        for each in (e_all, f_all, h_all, i_all):
            each(c).wait_send()
        gather_sent(*a_all(c))

    def phase_y(c):
        gather_sent(*j_all(c))

    def n_copy(c, f):
        dev = (
            (s, lax.rem(g + NG - 1, NG)),
            (s, lax.rem(g + 1, NG)),
            (lax.rem(s + NS - 1, NS), g),
            (lax.rem(s + 1, NS), g),
        )[f]
        return remote(fsend.at[c, f], f_recv.at[c, f ^ 1], n_ss.at[c, f], n_rs.at[c, f ^ 1], dev)

    def total_rows(c, lo, n):
        v = dot(cbas[lo : lo + n, :], chosen[c])
        cols = slice(c * W, (c + 1) * W)
        v = v + local[lo : lo + n, cols]
        d = dcol[lo : lo + n, :]
        if W > 128:
            d = jnp.concatenate([d] * (W // 128), axis=1)
        return v * d

    def phase_n(c):
        gather_end(*l_all(c))
        for k in range(NCB):
            for low in range(QB):
                v = sol2[c, bidx_s[0, k] * QB + low].astype(F32) * (cnt_s[0, 0] > k).astype(F32)
                at = k * CB + low * HB
                chosen[c, at : at + HB, :] = v.astype(BF)
        cols = slice(c * W, (c + 1) * W)
        for f in range(4):
            v = total_rows(c, f * CB, CB)
            out_ref[f * CB : (f + 1) * CB, cols] = v
            fsend[c, f] = v.astype(BF)
            n_copy(c, f).start()

    def phase_r(c):
        cols = slice(c * W, (c + 1) * W)
        for f in range(2, 4):
            out_ref[f * 256 : (f + 1) * 256, cols] = total_rows(c, f * 256, 256)

    def phase_o(c):
        cols = slice(c * W, (c + 1) * W)
        inside = (g > 0, g < NG - 1, s > 0, s < NS - 1)
        for f in range(4):
            n_copy(c, f ^ 1).wait_recv()
            at = slice(f * CB, (f + 1) * CB)
            v = f_recv[c, f].astype(F32) * inside[f].astype(F32)
            out_ref[at, cols] = out_ref[at, cols] + v

    phases = dict(
        a=phase_a, b=phase_b, w=phase_w, d=phase_d, s=phase_s, e=phase_e, f=phase_f, h=phase_h, i=phase_i,
        j=phase_j, g=phase_g, q=phase_q, t=phase_t, x=phase_x, y=phase_y, k=phase_k, l=phase_l, n=phase_n, r=phase_r, o=phase_o,
    )
    for name in ORDER:
        phases[name[0]](int(name[1]))

    for c in range(NCH):
        gather_sent(*l_all(c))
        for f in range(4):
            n_copy(c, f).wait_send()


def local(
    residual,
    dscale,
    local_inverse,
    coarse_basis,
    block_counts,
    block_index,
    level2_inverse,
    level2_basis,
    group_index,
    level3_inverse,
):
    vm = pltpu.VMEM
    dma = pltpu.SemaphoreType.DMA
    vmem = pl.BlockSpec(memory_space=pltpu.VMEM)
    hbm = pl.BlockSpec(memory_space=pltpu.HBM)
    ring_sem = dma((NCH, 4, 2, NH))
    piece_sem = dma((NCH, 4, 2, MB2 // PJ))
    one_sem = dma((NCH,))
    scratch = [
        pltpu.SMEM((1, 1), jnp.int32), pltpu.SMEM((1, NCB), jnp.int32), pltpu.SMEM((1, MB2), jnp.int32),
        vm((1, NL), F32), vm((NL, NR), F32), vm((NL, NL), BF), vm((NL, NCB * CB), BF), vm((OWN2, NB2 * CB), BF),
        vm((OWN2, MB2 * CB), BF), vm((SL, NB3 * CB), BF), dma((10,)),
        vm((NL, 128), F32), vm((NL, NR), BF), vm((NL, NR), F32), vm((1024, 1024), BF),
        vm((4 * SL, 1024), BF), vm((NG, SL, NB3 * SL), BF), vm((NG, SL, NB3 * SL), BF),
        dma(()), dma(()),
        pltpu.SMEM((2, NB2), jnp.int32), pltpu.SMEM((2, NB3), jnp.int32),
        vm((QB * NCB, HB, NR), BF), vm((NCH, NG * NH, HB, W), BF), vm((NCH, 2, NH, HB, W), BF),
        vm((NCH, 4, 2, NH, HB, W), BF), ring_sem, ring_sem,
        vm((NCH, NG * NH, HB, W), BF), ring_sem, ring_sem, vm((OWN2, NR), F32), vm((NCH, MB2, NG, SL, W), BF),
        vm((NCH, 2, MB2 // PJ, PJ, SL, W), BF), vm((NCH, 4, 2, MB2 // PJ, PJ, SL, W), BF), piece_sem, piece_sem,
        vm((NCH, MB2, SL, W), F32), vm((NCH, NB3, SL, W), BF), vm((NCH, NS, SL, W), BF), one_sem, one_sem,
        vm((NCH, NB3, SL, W), BF), one_sem, one_sem,
        vm((NCH, NG, SL, W), BF), vm((NCH, NG, SL, W), BF), one_sem, one_sem,
        vm((NCH, NB3, SL, W), BF), one_sem, one_sem,
        vm((NCH, MB2, NG, SL, W), BF), piece_sem, piece_sem,
        vm((NCH, NG * NH, HB, W), BF), ring_sem, ring_sem,
        vm((NCH, NCB * CB, W), BF), vm((NCH, 4, CB, W), BF), vm((NCH, 4, CB, W), BF),
        dma((NCH, 4)), dma((NCH, 4)),
    ]
    out = pl.pallas_call(
        kernel,
        out_shape=jax.ShapeDtypeStruct((NL, NR), F32),
        in_specs=[hbm] * 10,
        out_specs=vmem,
        scratch_shapes=scratch,
        name="bddc",
        compiler_params=pltpu.CompilerParams(
            collective_id=0, has_side_effects=True, vmem_limit_bytes=60 << 20
        ),
    )(
        block_counts.reshape(1, 1), block_index, group_index, dscale, residual[0], local_inverse[0],
        coarse_basis[0], level2_inverse[0], level2_basis[0], level3_inverse,
    )
    return out[None]


def solution(mesh):
    return jax.shard_map(
        local,
        mesh=mesh,
        in_specs=(
            P(("sub", "grp"), None, None),
            P(("sub", "grp"), None),
            P(("sub", "grp"), None, None),
            P(("sub", "grp"), None, None),
            P(("sub", "grp")),
            P(("sub", "grp"), None),
            P("sub", "grp", None),
            P("sub", "grp", None),
            P("sub", None),
            P(("sub", "grp"), None),
        ),
        out_specs=P(("sub", "grp"), None, None),
        check_vma=False,
    )
```
